128 devices in a mesh: gx: 16 (over z, y), gy: 8 (over x, core).
Axes of the slice: x: 4, y: 4, z: 4, core: 2. Of those that a mesh axis runs over, the one named last changes fastest.
Arguments:
- density: float32 [1, 1024, 4096], P(None, 'gy', 'gx'), may hold values from 0.5 to 4
- velocity: float32 [2, 1, 1024, 4096], P(None, None, 'gy', 'gx'), may hold values from -1 to 1
- energy: float32 [1, 1024, 4096], P(None, 'gy', 'gx'), may hold values from 0.5 to 3
- material: int32 [1, 1024, 4096], P(None, 'gy', 'gx'), may hold values from 0 to 2
- limiter: int32 [1, 1024, 4096], P(None, 'gy', 'gx'), may hold values 0 or 1
- owners: int32 [32768], P(('gx', 'gy')), may hold values from 0 to 15, as said below
- dest_tile: int32 [32768], P(('gx', 'gy')), may hold values from 0 to 255, as said below
- tile_shift: float32 [1, 1024], P(None, 'gy'), may hold values from 0.25 to 0.75
Outputs:
- remapped: float32 [4, 1, 1024, 4096], P(None, None, 'gy', 'gx')
The draws below stay inside these ranges and needn't reach their ends.
Inputs may be any that keep to these rules, and one draw needn't show every extreme that they name: `owners`: within a plane every mesh row of tiles is rotated along x as a whole by a whole number of tiles, at most 1 either way, and the rotation does not fall from one row to the next; so a tile's owner is its own gx index or the one next to it on either side (wrapping). No device sends more than 128 tiles to either neighbour, and in every draw some device sends exactly 128 to its left neighbour and some exactly 128 to its right one. `dest_tile`: numbered like the owner's own tiles; a destination lies in the tile's own plane and row, and every Eulerian tile is the destination of exactly one Lagrangian tile.
All inputs are finite; a program needn't handle non-finite values. No bound on the sum of `limiter` on one device may be relied on, other than what follows from the above.
Results may differ from the reference program's by a relative error of at most 0.0003.
Values sent between devices are 32-bit elements; how exact they have to be, the bound alone decides.
A program may use at most 64 MiB of HBM per device.

```python
import math
import jax
import jax.numpy as jnp

PLANES = 1
CY = 128
CX = 256
TILE = 128
NX = 4096
NY = 1024
TLAG = 256
TILES = 32768
N_GX = 16
N_GY = 8


def drift_rows(key):
    half_span = CX // TILE // 2
    middle_rows = NY - 2 * CY
    odds = max(2, middle_rows // (2 * half_span + 1))
    plane_keys = jax.random.split(jax.random.fold_in(key, 7321), PLANES)
    row_index = jnp.arange(NY).astype(jnp.int32)

    def one_plane(plane_key):
        draws = jax.random.randint(plane_key, (NY,), 0, odds)
        rising = jnp.where(draws == 0, 1, 0).astype(jnp.int32)
        rising = jnp.where((row_index >= CY) & (row_index < NY - CY), rising, 0)
        level = jnp.clip(jnp.cumsum(rising) - half_span, -half_span, half_span)
        return jnp.where(row_index >= NY - CY, half_span, level)
    return jax.vmap(one_plane)(plane_keys).astype(jnp.int32)


def tile_routes(key):
    rotation = drift_rows(key)
    segments = CX // TILE
    tile_cols = NX // TILE
    columns = jnp.arange(tile_cols).astype(jnp.int32)
    landing = (columns[None, None, :] + rotation[:, :, None]) % tile_cols
    owner_col = landing // segments
    plane_index = jnp.arange(PLANES).astype(jnp.int32)[:, None, None]
    row_index = (jnp.arange(NY).astype(jnp.int32) % CY)[None, :, None]
    local_tile = (plane_index * CY + row_index) * segments + landing % segments
    owner_col = owner_col.reshape(PLANES, N_GY, CY, N_GX, segments).transpose(3, 1, 0, 2, 4).reshape(TILES)
    local_tile = local_tile.reshape(PLANES, N_GY, CY, N_GX, segments).transpose(3, 1, 0, 2, 4).reshape(TILES)
    return (owner_col.astype(jnp.int32), local_tile.astype(jnp.int32))


def draw_owners(key, part):
    return tile_routes(key)[0]


def draw_dest_tile(key, part):
    return tile_routes(key)[1]


def set_ends(values, key, low, top_value):
    longest = values.shape.index(max(values.shape))
    spots = []
    for shift in (0, 1):
        where = [jax.random.randint(jax.random.fold_in(key, axis), (), 0, length) for axis, length in enumerate(values.shape)]
        where[longest] = (where[longest] + shift) % values.shape[longest]
        spots.append(tuple(where))
    return values.at[spots[0]].set(low).at[spots[1]].set(top_value)


def level_of(stream_key, shape, cuts, low, high):
    def one(position, shards_of):
        steps = jax.random.uniform(jax.random.fold_in(jax.random.fold_in(stream_key, 6), position), (shards_of,), jnp.float32, low / len(cuts), high / len(cuts))
        return jnp.repeat(jnp.exp(steps), shape[position] // shards_of).reshape((-1,) + (1,) * (len(shape) - position - 1))

    loudness = one(*cuts[0])
    for cut in cuts[1:]:
        loudness = loudness * one(*cut)
    return loudness


def setup_inputs(seed: int = 0) -> dict:
    key_list = jax.random.split(jax.random.key(seed), 9)
    density = jnp.clip(jnp.exp(math.log(4.0) - 2.0794415 * jax.random.uniform(key_list[0], (PLANES, NY, NX), jnp.float32) ** level_of(key_list[0], (PLANES, NY, NX), ((1, 8), (2, 16)), -0.2, 0.2)), 0.5, 4.0)
    velocity = jnp.clip(jax.random.uniform(key_list[1], (2, PLANES, NY, NX), jnp.float32, -1.0, 1.0) * level_of(key_list[1], (2, PLANES, NY, NX), ((2, 8), (3, 16)), -0.4, 0.0), -1.0, 1.0)
    energy = jnp.clip(0.5 + 2.5 * jax.random.uniform(key_list[2], (PLANES, NY, NX), jnp.float32) ** level_of(key_list[2], (PLANES, NY, NX), ((1, 8), (2, 16)), -0.2, 0.2), 0.5, 3.0)
    material = set_ends(jax.random.randint(key_list[3], (PLANES, NY, NX), 0, 3), jax.random.fold_in(key_list[3], 1), 0, 2).astype(jnp.int32)
    limiter = set_ends((jax.random.randint(key_list[4], (PLANES, NY, NX), 0, 2) < 1).astype(jnp.int32), jax.random.fold_in(key_list[4], 1), 0, 1)
    owners = draw_owners(jax.random.fold_in(key_list[8], 71), 0)
    dest_tile = draw_dest_tile(jax.random.fold_in(key_list[8], 71), 0)
    tile_shift = jnp.clip(0.25 + 0.5 * jax.random.uniform(key_list[7], (PLANES, NY), jnp.float32) ** level_of(key_list[7], (PLANES, NY), ((1, 8),), -0.2, 0.2), 0.25, 0.75)
    return dict(density=density, velocity=velocity, energy=energy, material=material, limiter=limiter, owners=owners, dest_tile=dest_tile, tile_shift=tile_shift)


time_step = 0.05

def heat_ratio(material):
    return jnp.where(material == 0, 1.4, jnp.where(material == 1, 5.0 / 3.0, 3.0)).astype(jnp.float32)

def corners(grid_field):
    return (grid_field[..., :-1, :-1], grid_field[..., :-1, 1:], grid_field[..., 1:, :-1], grid_field[..., 1:, 1:])

def node_velocity(impedance, pressure, speed_x, speed_y):
    weights = corners(impedance)
    pushes = corners(pressure)
    along_x = corners(speed_x)
    along_y = corners(speed_y)
    totals = weights[0] + weights[1] + weights[2] + weights[3]
    moment_x = weights[0] * along_x[0] + weights[1] * along_x[1] + weights[2] * along_x[2] + weights[3] * along_x[3]
    moment_y = weights[0] * along_y[0] + weights[1] * along_y[1] + weights[2] * along_y[2] + weights[3] * along_y[3]
    node_x = (moment_x + (pushes[0] - pushes[1] + pushes[2] - pushes[3])) / totals
    node_y = (moment_y + (pushes[0] + pushes[1] - pushes[2] - pushes[3])) / totals
    return (node_x, node_y)

def cell_update(impedance, pressure, speed_x, speed_y, density, energy_total, node_x, node_y):
    nodes_x = corners(node_x)
    nodes_y = corners(node_y)
    sum_x = nodes_x[0] + nodes_x[1] + nodes_x[2] + nodes_x[3]
    sum_y = nodes_y[0] + nodes_y[1] + nodes_y[2] + nodes_y[3]
    force_x = 0.5 * impedance * (sum_x - 4.0 * speed_x)
    force_y = 0.5 * impedance * (sum_y - 4.0 * speed_y)
    volume_rate = 0.5 * (-nodes_x[0] - nodes_y[0] + nodes_x[1] - nodes_y[1] - nodes_x[2] + nodes_y[2] + nodes_x[3] + nodes_y[3])
    relaxation = jnp.zeros_like(speed_x)
    for corner in range(4):
        relaxation = relaxation + (nodes_x[corner] - speed_x) * nodes_x[corner] + (nodes_y[corner] - speed_y) * nodes_y[corner]
    work_rate = -pressure * volume_rate + 0.5 * impedance * relaxation
    conserved = jnp.stack([density, density * speed_x + time_step * force_x, density * speed_y + time_step * force_y, energy_total + time_step * work_rate])
    left_speed = 0.5 * (nodes_x[0] + nodes_x[2])
    right_speed = 0.5 * (nodes_x[1] + nodes_x[3])
    widths = 1.0 + time_step * (right_speed - left_speed)
    return (conserved / widths, left_speed, right_speed)

def minmod(left_side, right_side):
    return jnp.where(left_side * right_side > 0, jnp.sign(left_side) * jnp.minimum(jnp.abs(left_side), jnp.abs(right_side)), 0.0)

def centred(left_side, right_side):
    limit_mag = jnp.minimum(jnp.minimum(2.0 * jnp.abs(left_side), 2.0 * jnp.abs(right_side)), 0.5 * jnp.abs(left_side + right_side))
    return jnp.where(left_side * right_side > 0, jnp.sign(left_side) * limit_mag, 0.0)

def limited(values, neighbour_left, neighbour_right, limiter):
    widened = jnp.concatenate([neighbour_left, values, neighbour_right], axis=-1)
    back_diff = values - widened[..., :-2]
    fore_diff = widened[..., 2:] - values
    return jnp.where(limiter == 1, centred(back_diff, fore_diff), minmod(back_diff, fore_diff))

def integrate(values, slopes, left_pos, right_pos):
    cell_pos = jnp.arange(values.shape[-1]).astype(jnp.float32)
    centre = 0.5 * (left_pos + right_pos)
    low_own = jnp.maximum(left_pos, cell_pos)
    high_own = jnp.minimum(right_pos, cell_pos + 1.0)
    span_own = jnp.maximum(high_own - low_own, 0.0)
    offset_own = 0.5 * (high_own + low_own) - centre
    low_next = jnp.maximum(left_pos, cell_pos + 1.0)
    high_next = jnp.minimum(right_pos, cell_pos + 2.0)
    span_next = jnp.maximum(high_next - low_next, 0.0)
    offset_next = 0.5 * (high_next + low_next) - centre
    part_own = span_own[..., None, :] * (values + slopes * offset_own[..., None, :])
    part_next = span_next[..., None, :] * (values + slopes * offset_next[..., None, :])
    empty_col = jnp.zeros_like(part_next[..., :1])
    main_part = part_own + jnp.concatenate([empty_col, part_next[..., :-1]], axis=-1)
    return (main_part, part_next[..., -1])

def reference(density, velocity, energy, material, limiter, owners, dest_tile, tile_shift):
    segments = CX // TILE
    ratios = heat_ratio(material)
    pressure = (ratios - 1.0) * density * energy
    impedance = density * jnp.sqrt(ratios * (ratios - 1.0) * energy)
    speed_x = velocity[0]
    speed_y = velocity[1]
    energy_total = density * (energy + 0.5 * (speed_x * speed_x + speed_y * speed_y))
    stacked = jnp.stack([impedance, pressure, speed_x, speed_y])
    padded = jnp.pad(stacked, ((0, 0), (0, 0), (1, 1), (0, 0)))
    padded = jnp.concatenate([padded[..., -1:], padded, padded[..., :1]], axis=-1)
    node_x, node_y = node_velocity(padded[0], padded[1], padded[2], padded[3])
    values, left_speed, right_speed = cell_update(impedance, pressure, speed_x, speed_y, density, energy_total, node_x, node_y)
    slopes = limited(values, values[..., -1:], values[..., :1], limiter)

    def field_tiles(source_field):
        return source_field.reshape(4, PLANES, N_GY, CY, N_GX, segments, TILE).transpose(4, 2, 1, 3, 5, 0, 6).reshape(TILES, 4, TILE)

    def plain_tiles(source_field):
        return source_field.reshape(PLANES, N_GY, CY, N_GX, segments, TILE).transpose(3, 1, 0, 2, 4, 5).reshape(TILES, TILE)
    cell_pos = jnp.arange(TILE).astype(jnp.float32)
    offsets = plain_tiles(jnp.broadcast_to(tile_shift[:, :, None], (PLANES, NY, NX)))[:, :1]
    left_pos = cell_pos + offsets + time_step * plain_tiles(left_speed)
    right_pos = cell_pos + 1.0 + offsets + time_step * plain_tiles(right_speed)
    main_part, spill_part = integrate(field_tiles(values), field_tiles(slopes), left_pos, right_pos)
    tile_ids = jnp.arange(TILES).astype(jnp.int32)
    band_index = tile_ids // TLAG % N_GY
    targets = ((owners * N_GY + band_index) * TLAG + dest_tile).astype(jnp.int32)
    at_end = dest_tile % segments == segments - 1
    next_owner = (owners + 1) % N_GX
    spill_targets = jnp.where(at_end, (next_owner * N_GY + band_index) * TLAG + dest_tile - (segments - 1), targets + 1).astype(jnp.int32)
    gathered = jax.ops.segment_sum(main_part, targets, num_segments=TILES)
    spilled = jax.ops.segment_sum(spill_part, spill_targets, num_segments=TILES)
    gathered = gathered.at[:, :, 0].add(spilled)
    return gathered.reshape(N_GX, N_GY, PLANES, CY, segments, 4, TILE).transpose(5, 2, 1, 3, 0, 4, 6).reshape(4, PLANES, NY, NX)
```

```python
import functools

import jax
import jax.numpy as jnp
from jax import lax
from jax.experimental import pallas as pl
from jax.experimental.pallas import tpu as pltpu
from jax.sharding import PartitionSpec as P

MESH = pl.DeviceIdType.MESH
TILE = 128
ROWS = 128
COLS = 256
PAD = 8
G = 8
time_step = 0.05

RUNS = ((1, 5), (5, 9), (9, 13), (13, 15))


def by_material(material, first, second, third):
    return jnp.where(material == 0, first, jnp.where(material == 1, second, third))


def cell_state(density, energy, material):
    pressure = by_material(material, 0.4, 2.0 / 3.0, 2.0) * density * energy
    squared = by_material(material, 0.56, 10.0 / 9.0, 6.0) * energy
    return density * jnp.sqrt(squared), pressure


def node_speed(low, high, left):
    weight = low[0] + high[0]
    from_left = low[1] + high[1]
    from_right = low[2] + high[2]
    along_y = low[3] + high[3]
    scale = 1.0 / (left(weight) + weight)
    return (left(from_left) + from_right) * scale, (left(along_y) + along_y) * scale


def remap_parts(density, energy, speed_x, speed_y, impedance, pressure, limiter, nodes, shift, mask, left, right):
    low_x, low_y, high_x, high_y = nodes
    edge_x = low_x + high_x
    edge_y = low_y + high_y
    turn_y = high_y - low_y
    square = low_x * low_x + high_x * high_x + low_y * low_y + high_y * high_y
    next_x = right(edge_x)
    sum_x = edge_x + next_x
    sum_y = edge_y + right(edge_y)
    volume_rate = 0.5 * ((next_x - edge_x) + (turn_y + right(turn_y)))
    relaxation = (square + right(square)) - speed_x * sum_x - speed_y * sum_y
    half = 0.5 * impedance
    work = half * relaxation - pressure * volume_rate
    left_move = (0.5 * time_step) * edge_x
    right_move = (0.5 * time_step) * next_x
    scale = 1.0 / (1.0 + (right_move - left_move))
    total = density * (energy + 0.5 * (speed_x * speed_x + speed_y * speed_y))
    conserved = (
        density,
        density * speed_x + (time_step * half) * (sum_x - 4.0 * speed_x),
        density * speed_y + (time_step * half) * (sum_y - 4.0 * speed_y),
        total + time_step * work,
    )
    reach = jnp.where(limiter == 1, 2.0, 1.0)
    left_pos = shift + left_move
    right_pos = 1.0 + shift + right_move
    centre = 0.5 * (left_pos + right_pos)
    low_own = jnp.maximum(left_pos, 0.0)
    high_own = jnp.minimum(right_pos, 1.0)
    span_own = jnp.where(mask, jnp.maximum(high_own - low_own, 0.0), 0.0)
    offset_own = 0.5 * (high_own + low_own) - centre
    low_next = jnp.maximum(left_pos, 1.0)
    high_next = jnp.minimum(right_pos, 2.0)
    span_next = jnp.where(mask, jnp.maximum(high_next - low_next, 0.0), 0.0)
    offset_next = 0.5 * (high_next + low_next) - centre
    sums = []
    for field in conserved:
        value = field * scale
        back = value - left(value)
        fore = right(back)
        half_sum = 0.5 * (back + fore)
        limit = reach * jnp.minimum(jnp.abs(back), jnp.abs(fore))
        slope = jnp.where(back * fore > 0.0, jnp.maximum(jnp.minimum(half_sum, limit), -limit), 0.0)
        part_own = span_own * (value + slope * offset_own)
        part_next = span_next * (value + slope * offset_next)
        sums.append(part_own + left(part_next))
    return sums


def kernel(
    n_gx, n_gy,
    density_in, velocity_in, energy_in, material_in, limiter_in, owners_ref, dest_ref, shift_ref, out_ref,
    rho, spx, spy, ene, mat, lim, zed, pre, pl_x, pr_x, pl_y, pu_y, node_x, node_y, shift_b, turn_b,
    to_left, to_right, from_left, from_right, base, outer_up, outer_down, from_down, from_up,
    seam_out_l, seam_out_r, seam_in_l, seam_in_r, rim,
    in_sem, out_sem, bulk_send, bulk_recv, row_send, row_recv, seam_send, seam_recv,
):
    gx = lax.axis_index("gx")
    gy = lax.axis_index("gy")
    right_x = lax.rem(gx + 1, n_gx)
    left_x = lax.rem(gx + n_gx - 1, n_gx)
    up_y = lax.rem(gy + 1, n_gy)
    down_y = lax.rem(gy + n_gy - 1, n_gy)

    loads = [
        pltpu.make_async_copy(source, target, in_sem.at[i])
        for i, (source, target) in enumerate(
            (
                (density_in.at[0], rho),
                (energy_in.at[0], ene),
                (material_in.at[0], mat),
                (velocity_in.at[0, 0], spx),
                (velocity_in.at[1, 0], spy),
                (limiter_in.at[0], lim),
            )
        )
    ]
    for load in loads:
        load.start()

    barrier = pltpu.get_barrier_semaphore()
    for target in ((left_x, gy), (right_x, gy), (gx, up_y), (gx, down_y)):
        pl.semaphore_signal(barrier, inc=1, device_id=target, device_id_type=MESH)

    lanes = lax.broadcasted_iota(jnp.int32, (ROWS, TILE), 1)
    rows = lax.broadcasted_iota(jnp.int32, (ROWS, TILE), 0)

    turn_pairs = jnp.where(owners_ref[...] == gx, lax.bitwise_and(dest_ref[...], 1), -1).astype(jnp.float32)
    turn_row = jnp.zeros((8, ROWS), jnp.float32)
    for j in range(2):
        pick = jnp.where(TILE * j + rows == 2 * lanes, 1.0, 0.0)
        turn_row += jnp.dot(
            jnp.broadcast_to(turn_pairs[j : j + 1], (8, TILE)), pick, preferred_element_type=jnp.float32
        )
    turn_row = turn_row[0:1]
    turn_b[...] = jnp.transpose(jnp.broadcast_to(turn_row, (ROWS, ROWS)))
    shift_row = shift_ref[...]
    shift_b[...] = jnp.transpose(jnp.broadcast_to(shift_row, (ROWS, ROWS)))

    def wide(ref, start):
        return jnp.concatenate([ref[0, pl.ds(start, G), :], ref[1, pl.ds(start, G), :]], axis=1)

    def keep(ref, start, value):
        ref[0, pl.ds(start, G), :] = value[:, :TILE]
        ref[1, pl.ds(start, G), :] = value[:, TILE:]

    def left(x):
        return pltpu.roll(x, 1, 1)

    def right(x):
        return pltpu.roll(x, COLS - 1, 1)

    def derive(g, carry=None):
        at = pl.multiple_of(g * G, G)
        density = rho[pl.ds(at, G), :]
        speed_x = spx[pl.ds(at, G), :]
        speed_y = spy[pl.ds(at, G), :]
        impedance, pressure = cell_state(density, ene[pl.ds(at, G), :], mat[pl.ds(at, G), :])
        pad_at = pl.multiple_of(at + PAD, G)
        keep(zed, pad_at, impedance)
        pre[pl.ds(at, G), :] = pressure
        push_x = impedance * speed_x
        push_y = impedance * speed_y
        keep(pl_x, pad_at, push_x + pressure)
        keep(pr_x, pad_at, push_x - pressure)
        keep(pl_y, pad_at, push_y + pressure)
        keep(pu_y, pad_at, push_y - pressure)
        return carry

    def nodes(g, carry=None):
        at = pl.multiple_of(g * G, G)
        low = [wide(ref, at + PAD - 1) for ref in (zed, pl_x, pr_x, pl_y)]
        high = [wide(ref, pl.multiple_of(at + PAD, G)) for ref in (zed, pl_x, pr_x, pu_y)]
        x, y = node_speed(low, high, left)
        keep(node_x, at, x)
        keep(node_y, at, y)
        return carry

    inner = lax.broadcasted_iota(jnp.int32, (G, COLS), 1)
    inner = (inner >= 2) & (inner < COLS - 2)

    def cells(g, carry=None):
        at = pl.multiple_of(g * G, G)
        here = pl.ds(at, G)
        near = [wide(node_x, at), wide(node_y, at), wide(node_x, at + 1), wide(node_y, at + 1)]
        shift = shift_b[here, :]
        sums = remap_parts(
            rho[here, :], ene[here, :], spx[here, :], spy[here, :],
            wide(zed, pl.multiple_of(at + PAD, G)), pre[here, :], lim[here, :], near,
            jnp.concatenate([shift, shift], axis=1), inner, left, right,
        )
        for f in range(4):
            to_left[f, here, :] = sums[f][:, :TILE]
            to_right[f, here, :] = sums[f][:, TILE:]
        return carry

    def over(first, last, step):
        lax.fori_loop(first, last, step, None)

    sends = []

    def send_rows(i, first, count):
        there = pl.ds(first * G, count * G)
        for way, (source, target, device) in enumerate(
            ((to_right, from_left, right_x), (to_left, from_right, left_x))
        ):
            copy = pltpu.make_async_remote_copy(
                src_ref=source.at[:, there, :],
                dst_ref=target.at[:, there, :],
                send_sem=bulk_send.at[way, i],
                recv_sem=bulk_recv.at[way, i],
                device_id=(device, gy),
                device_id_type=MESH,
            )
            copy.start()
            sends.append(copy)

    for load in loads:
        load.wait()

    filler = jnp.ones((G, TILE), jnp.float32)
    for ref in (zed, pl_x, pr_x, pl_y, pu_y):
        for half in range(2):
            ref[half, 0:G, :] = filler
            ref[half, ROWS + PAD : ROWS + PAD + G, :] = filler

    derive(15)
    over(0, 6, derive)
    over(1, 6, nodes)

    for half in range(2):
        for k, ref in enumerate((zed, pl_x, pr_x, pl_y)):
            outer_up[4 * half + k : 4 * half + k + 1, :] = ref[half, ROWS + PAD - 1 : ROWS + PAD, :]
        for k, ref in enumerate((zed, pl_x, pr_x, pu_y)):
            outer_down[4 * half + k : 4 * half + k + 1, :] = ref[half, PAD : PAD + 1, :]

    over(1, 5, cells)

    pl.semaphore_wait(barrier, 4)

    row_copies = []
    for way, (source, target, device) in enumerate(((outer_up, from_down, up_y), (outer_down, from_up, down_y))):
        copy = pltpu.make_async_remote_copy(
            src_ref=source, dst_ref=target, send_sem=row_send.at[way], recv_sem=row_recv.at[way],
            device_id=(gx, device), device_id_type=MESH,
        )
        copy.start()
        row_copies.append(copy)

    send_rows(0, 1, 4)
    for i, (first, last) in enumerate(RUNS[1:3]):
        top = min(last + 1, 15)
        over(first + 1, top, derive)
        over(first + 1, last + 1, nodes)
        over(first, last, cells)
        send_rows(1 + i, first, last - first)
    over(14, 15, derive)
    over(14, 16, nodes)
    over(13, 15, cells)

    packed_l = jnp.zeros((ROWS, TILE), jnp.float32)
    packed_r = jnp.zeros((ROWS, TILE), jnp.float32)
    for f, ref in enumerate((rho, ene, spx, spy, mat, lim)):
        first = ref[:, :TILE].astype(jnp.float32)
        last = ref[:, TILE:].astype(jnp.float32)
        inside = (lanes >= 4 * f) & (lanes < 4 * f + 4)
        packed_l = jnp.where(inside, pltpu.roll(first, 4 * f, 1) if f else first, packed_l)
        packed_r = jnp.where(inside, pltpu.roll(last, 4 * f + 4, 1), packed_r)
    seam_out_l[0:24, :] = jnp.transpose(packed_l)[0:24, :]
    seam_out_r[0:24, :] = jnp.transpose(packed_r)[0:24, :]

    for copy in row_copies:
        copy.wait()
    below = jnp.where(gy == 0, 0.0, from_down[...])
    above = jnp.where(gy == n_gy - 1, 0.0, from_up[...])
    for half in range(2):
        for k, ref in enumerate((zed, pl_x, pr_x, pl_y)):
            ref[half, PAD - 1 : PAD, :] = below[4 * half + k : 4 * half + k + 1, :]
        for k, ref in enumerate((zed, pl_x, pr_x, pu_y)):
            ref[half, ROWS + PAD : ROWS + PAD + 1, :] = above[4 * half + k : 4 * half + k + 1, :]
    outer_turned = jnp.transpose(
        jnp.concatenate([below, above, jnp.zeros((ROWS - 16, TILE), jnp.float32)], axis=0)
    )
    seam_out_l[24:32, :] = outer_turned[0:8, :]
    seam_out_r[24:32, :] = outer_turned[120:128, :]

    seam_copies = []
    for way, (source, target, device) in enumerate(
        ((seam_out_r, seam_in_l, right_x), (seam_out_l, seam_in_r, left_x))
    ):
        copy = pltpu.make_async_remote_copy(
            src_ref=source, dst_ref=target, send_sem=seam_send.at[way], recv_sem=seam_recv.at[way],
            device_id=(device, gy), device_id_type=MESH,
        )
        copy.start()
        seam_copies.append(copy)
    send_rows(3, 13, 2)
    nodes(0)
    nodes(16)
    cells(0)
    cells(15)
    send_rows(4, 0, 1)
    send_rows(5, 15, 1)

    for copy in seam_copies:
        copy.wait()

    sub8 = lax.broadcasted_iota(jnp.int32, (8, TILE), 0)
    lane8 = lax.broadcasted_iota(jnp.int32, (8, TILE), 1)

    def turned(x, by):
        return pltpu.roll(x, by % 8, 0) if by % 8 else x

    def seam_field(f):
        at, off = 8 * (f // 2), 4 * (f % 2)
        slots = []
        for before, after in ((seam_in_l, seam_out_l), (seam_out_r, seam_in_r)):
            head = turned(before[at : at + 8, :], 8 - off)
            tail = turned(after[at : at + 8, :], 4 - off + 8)
            slots.append(jnp.where(sub8 < 4, head, tail))
        return jnp.concatenate(slots, axis=0)

    def seam_outer(column):
        slots = []
        for before, after, b_off in ((seam_in_l, seam_out_l, 4), (seam_out_r, seam_in_r, 4)):
            head = turned(before[24:32, :], b_off)
            tail = turned(after[24:32, :], 4)
            slots.append(jnp.where(sub8 < 4, head, tail)[:, column : column + 1])
        return jnp.concatenate(slots, axis=0)

    density, energy, speed_x, speed_y, material, limiter = [seam_field(f) for f in range(6)]
    impedance, pressure = cell_state(density, energy, material)
    push_x = impedance * speed_x
    push_y = impedance * speed_y
    first_lane = lax.broadcasted_iota(jnp.int32, (16, ROWS), 1)
    at_first = first_lane == 0
    at_last = first_lane == ROWS - 1

    is_before = lax.broadcasted_iota(jnp.int32, (16, 1), 0)
    is_before = lax.rem(is_before, 8) < 4

    def outer_value(k):
        return jnp.where(is_before, seam_outer(4 + k), seam_outer(k))

    mine_l = (impedance, push_x + pressure, push_x - pressure, push_y + pressure)
    mine_u = (impedance, push_x + pressure, push_x - pressure, push_y - pressure)
    under = [jnp.where(at_first, outer_value(k), pltpu.roll(x, 1, 1)) for k, x in enumerate(mine_l)]
    over_it = [jnp.where(at_last, outer_value(8 + k), pltpu.roll(x, ROWS - 1, 1)) for k, x in enumerate(mine_u)]

    def seam_left(x):
        return pltpu.roll(x, 1, 0)

    def seam_right(x):
        return pltpu.roll(x, 15, 0)

    low = node_speed(under, mine_u, seam_left)
    high = node_speed(mine_l, over_it, seam_left)
    sub16 = lax.rem(lax.broadcasted_iota(jnp.int32, (16, ROWS), 0), 8)
    sums = remap_parts(
        density, energy, speed_x, speed_y, impedance, pressure, limiter, low + high,
        jnp.broadcast_to(shift_row, (16, ROWS)), (sub16 >= 2) & (sub16 < 6), seam_left, seam_right,
    )
    stay = turn_row == 0.0
    goes_right = turn_row == 1.0
    goes_left = turn_row == -1.0
    pieces = []
    for f in range(4):
        at_left, at_right = sums[f][0:8], sums[f][8:16]
        moved = jnp.where(goes_right, at_left, jnp.where(goes_left, at_right, 0.0))
        pieces.append(jnp.where(sub8 < 4, moved, jnp.where(stay, at_left, 0.0)))
        pieces.append(jnp.where(sub8 < 4, jnp.where(stay, at_right, 0.0), moved))
    rim[...] = jnp.transpose(jnp.concatenate(pieces + [jnp.zeros((64, ROWS), jnp.float32)], axis=0))

    near_edge = (lane8 < 3) | (lane8 >= TILE - 2)

    def prepare(g, carry):
        here = pl.ds(pl.multiple_of(g * G, G), G)
        turn = turn_b[here, :]
        edge = rim[here, :]
        for f in range(4):
            first, second = to_left[f, here, :], to_right[f, here, :]
            for half in range(2):
                q = 2 * f + half
                if half == 0:
                    value = jnp.where(turn == 0.0, first, jnp.where(turn == 1.0, 0.0, second))
                else:
                    value = jnp.where(turn == 0.0, second, jnp.where(turn == 1.0, first, 0.0))
                extra = pltpu.roll(edge, (2 * TILE - 8 * q - 4) % TILE, 1)
                base[f, here, half * TILE : (half + 1) * TILE] = value + jnp.where(near_edge, extra, 0.0)
        return carry

    def finish(g, carry=None):
        here = pl.ds(pl.multiple_of(g * G, G), G)
        turn = turn_b[here, :]
        for f in range(4):
            base[f, here, :TILE] += jnp.where(turn == 1.0, from_left[f, here, :], 0.0)
            base[f, here, TILE:] += jnp.where(turn == -1.0, from_right[f, here, :], 0.0)
        return carry

    over(0, 16, prepare)

    outs = []
    for i, (first, last) in enumerate(((1, 5), (5, 9), (9, 13), (13, 15), (0, 1), (15, 16))):
        sends[2 * i].wait()
        sends[2 * i + 1].wait()
        over(first, last, finish)
        there = pl.ds(first * G, (last - first) * G)
        out = pltpu.make_async_copy(base.at[:, there, :], out_ref.at[:, 0, there, :], out_sem.at[i])
        out.start()
        outs.append(out)
    for out in outs:
        out.wait()


def on_device(n_gx, n_gy, density, velocity, energy, material, limiter, owners, dest_tile, tile_shift):
    dma = pltpu.SemaphoreType.DMA
    f32 = jnp.float32
    block = pltpu.VMEM((ROWS, COLS), f32)
    padded = pltpu.VMEM((2, ROWS + 2 * PAD, TILE), f32)
    tiles = pltpu.VMEM((4, ROWS, TILE), f32)
    square = pltpu.VMEM((ROWS, TILE), f32)
    small = pltpu.VMEM((8, TILE), f32)
    seam = pltpu.VMEM((32, ROWS), f32)
    any_space = pl.BlockSpec(memory_space=pl.ANY)
    vmem = pl.BlockSpec(memory_space=pltpu.VMEM)
    return pl.pallas_call(
        functools.partial(kernel, n_gx, n_gy),
        out_shape=jax.ShapeDtypeStruct((4, 1, ROWS, COLS), f32),
        in_specs=[any_space] * 5 + [vmem] * 3,
        out_specs=any_space,
        scratch_shapes=[
            block, block, block, block,
            pltpu.VMEM((ROWS, COLS), jnp.int32), pltpu.VMEM((ROWS, COLS), jnp.int32),
            padded, block, padded, padded, padded, padded, padded, padded, square, square,
            tiles, tiles, tiles, tiles, pltpu.VMEM((4, ROWS, COLS), f32),
            small, small, small, small, seam, seam, seam, seam, square,
            dma((6,)), dma((6,)), dma((2, 6)), dma((2, 6)), dma((2,)), dma((2,)), dma((2,)), dma((2,)),
        ],
        compiler_params=pltpu.CompilerParams(
            collective_id=0, has_side_effects=True, vmem_limit_bytes=24 * 1024 * 1024
        ),
    )(
        density, velocity, energy, material, limiter,
        owners.reshape(2, TILE), dest_tile.reshape(2, TILE), tile_shift,
    )


def solution(mesh):
    placed = (
        P(None, "gy", "gx"),
        P(None, None, "gy", "gx"),
        P(None, "gy", "gx"),
        P(None, "gy", "gx"),
        P(None, "gy", "gx"),
        P(("gx", "gy")),
        P(("gx", "gy")),
        P(None, "gy"),
    )
    return jax.shard_map(
        functools.partial(on_device, mesh.shape["gx"], mesh.shape["gy"]),
        mesh=mesh, in_specs=placed, out_specs=P(None, None, "gy", "gx"), check_vma=False,
    )
```

```python
import functools

import jax
import jax.numpy as jnp
from jax import lax
from jax.experimental import pallas as pl
from jax.experimental.pallas import tpu as pltpu
from jax.sharding import PartitionSpec as P

MESH = pl.DeviceIdType.MESH
TILE = 128
ROWS = 128
COLS = 256
PAD = 8
G = 8
time_step = 0.05

RUNS = ((1, 5), (5, 9), (9, 13), (13, 15))


def by_material(material, first, second, third):
    return jnp.where(material == 0, first, jnp.where(material == 1, second, third))


def cell_state(density, energy, material):
    pressure = by_material(material, 0.4, 2.0 / 3.0, 2.0) * density * energy
    squared = by_material(material, 0.56, 10.0 / 9.0, 6.0) * energy
    return density * jnp.sqrt(squared), pressure


def node_speed(low, high, left):
    weight = low[0] + high[0]
    from_left = low[1] + high[1]
    from_right = low[2] + high[2]
    along_y = low[3] + high[3]
    scale = 1.0 / (left(weight) + weight)
    return (left(from_left) + from_right) * scale, (left(along_y) + along_y) * scale


def remap_parts(density, energy, speed_x, speed_y, impedance, pressure, limiter, nodes, shift, mask, left, right):
    low_x, low_y, high_x, high_y = nodes
    edge_x = low_x + high_x
    edge_y = low_y + high_y
    turn_y = high_y - low_y
    square = low_x * low_x + high_x * high_x + low_y * low_y + high_y * high_y
    next_x = right(edge_x)
    sum_x = edge_x + next_x
    sum_y = edge_y + right(edge_y)
    volume_rate = 0.5 * ((next_x - edge_x) + (turn_y + right(turn_y)))
    relaxation = (square + right(square)) - speed_x * sum_x - speed_y * sum_y
    half = 0.5 * impedance
    work = half * relaxation - pressure * volume_rate
    left_move = (0.5 * time_step) * edge_x
    right_move = (0.5 * time_step) * next_x
    scale = 1.0 / (1.0 + (right_move - left_move))
    total = density * (energy + 0.5 * (speed_x * speed_x + speed_y * speed_y))
    conserved = (
        density,
        density * speed_x + (time_step * half) * (sum_x - 4.0 * speed_x),
        density * speed_y + (time_step * half) * (sum_y - 4.0 * speed_y),
        total + time_step * work,
    )
    reach = jnp.where(limiter == 1, 2.0, 1.0)
    left_pos = shift + left_move
    right_pos = 1.0 + shift + right_move
    centre = 0.5 * (left_pos + right_pos)
    low_own = jnp.maximum(left_pos, 0.0)
    high_own = jnp.minimum(right_pos, 1.0)
    span_own = jnp.where(mask, jnp.maximum(high_own - low_own, 0.0), 0.0)
    offset_own = 0.5 * (high_own + low_own) - centre
    low_next = jnp.maximum(left_pos, 1.0)
    high_next = jnp.minimum(right_pos, 2.0)
    span_next = jnp.where(mask, jnp.maximum(high_next - low_next, 0.0), 0.0)
    offset_next = 0.5 * (high_next + low_next) - centre
    sums = []
    for field in conserved:
        value = field * scale
        back = value - left(value)
        fore = right(back)
        half_sum = 0.5 * (back + fore)
        limit = reach * jnp.minimum(jnp.abs(back), jnp.abs(fore))
        slope = jnp.where(back * fore > 0.0, jnp.maximum(jnp.minimum(half_sum, limit), -limit), 0.0)
        part_own = span_own * (value + slope * offset_own)
        part_next = span_next * (value + slope * offset_next)
        sums.append(part_own + left(part_next))
    return sums


def kernel(
    n_gx, n_gy,
    density_in, velocity_in, energy_in, material_in, limiter_in, owners_in, dest_in, shift_in, out_ref,
    owners_ref, dest_ref, shift_ref, rho, spx, spy, ene, mat, lim, zed, pre, pl_x, pr_x, pl_y, pu_y, node_x, node_y, shift_b, turn_b,
    to_left, to_right, from_left, from_right, outer_up, outer_down, from_down, from_up,
    seam_out_l, seam_out_r, seam_in_l, seam_in_r, rim,
    in_sem, bulk_send, bulk_recv, row_send, row_recv, seam_send, seam_recv,
):
    gx = lax.axis_index("gx")
    gy = lax.axis_index("gy")
    right_x = lax.rem(gx + 1, n_gx)
    left_x = lax.rem(gx + n_gx - 1, n_gx)
    up_y = lax.rem(gy + 1, n_gy)
    down_y = lax.rem(gy + n_gy - 1, n_gy)

    loads = [
        pltpu.make_async_copy(source, target, in_sem.at[i])
        for i, (source, target) in enumerate(
            (
                (density_in.at[0], rho),
                (energy_in.at[0], ene),
                (material_in.at[0], mat),
                (velocity_in.at[0, 0], spx),
                (velocity_in.at[1, 0], spy),
                (limiter_in.at[0], lim),
                (owners_in, owners_ref),
                (dest_in, dest_ref),
                (shift_in, shift_ref),
            )
        )
    ]
    for load in loads:
        load.start()

    barrier = pltpu.get_barrier_semaphore()
    for target in ((left_x, gy), (right_x, gy), (gx, up_y), (gx, down_y)):
        pl.semaphore_signal(barrier, inc=1, device_id=target, device_id_type=MESH)

    lanes = lax.broadcasted_iota(jnp.int32, (ROWS, TILE), 1)
    rows = lax.broadcasted_iota(jnp.int32, (ROWS, TILE), 0)

    def wide(ref, start):
        return jnp.concatenate([ref[0, pl.ds(start, G), :], ref[1, pl.ds(start, G), :]], axis=1)

    def keep(ref, start, value):
        ref[0, pl.ds(start, G), :] = value[:, :TILE]
        ref[1, pl.ds(start, G), :] = value[:, TILE:]

    def left(x):
        return pltpu.roll(x, 1, 1)

    def right(x):
        return pltpu.roll(x, COLS - 1, 1)

    def derive(g, carry=None):
        at = pl.multiple_of(g * G, G)
        density = rho[pl.ds(at, G), :]
        speed_x = spx[pl.ds(at, G), :]
        speed_y = spy[pl.ds(at, G), :]
        impedance, pressure = cell_state(density, ene[pl.ds(at, G), :], mat[pl.ds(at, G), :])
        pad_at = pl.multiple_of(at + PAD, G)
        keep(zed, pad_at, impedance)
        pre[pl.ds(at, G), :] = pressure
        push_x = impedance * speed_x
        push_y = impedance * speed_y
        keep(pl_x, pad_at, push_x + pressure)
        keep(pr_x, pad_at, push_x - pressure)
        keep(pl_y, pad_at, push_y + pressure)
        keep(pu_y, pad_at, push_y - pressure)
        return carry

    def nodes(g, carry=None):
        at = pl.multiple_of(g * G, G)
        low = [wide(ref, at + PAD - 1) for ref in (zed, pl_x, pr_x, pl_y)]
        high = [wide(ref, pl.multiple_of(at + PAD, G)) for ref in (zed, pl_x, pr_x, pu_y)]
        x, y = node_speed(low, high, left)
        keep(node_x, at, x)
        keep(node_y, at, y)
        return carry

    inner = lax.broadcasted_iota(jnp.int32, (G, COLS), 1)
    inner = (inner >= 2) & (inner < COLS - 2)

    def cells(g, carry=None):
        at = pl.multiple_of(g * G, G)
        here = pl.ds(at, G)
        near = [wide(node_x, at), wide(node_y, at), wide(node_x, at + 1), wide(node_y, at + 1)]
        shift = shift_b[here, :]
        sums = remap_parts(
            rho[here, :], ene[here, :], spx[here, :], spy[here, :],
            wide(zed, pl.multiple_of(at + PAD, G)), pre[here, :], lim[here, :], near,
            jnp.concatenate([shift, shift], axis=1), inner, left, right,
        )
        for f in range(4):
            to_left[f, here, :] = sums[f][:, :TILE]
            to_right[f, here, :] = sums[f][:, TILE:]
        return carry

    def over(first, last, step):
        lax.fori_loop(first, last, step, None, unroll=min(4, last - first))

    sends = []

    def send_rows(i, first, count):
        there = pl.ds(first * G, count * G)
        for way, (source, target, device) in enumerate(
            ((to_right, from_left, right_x), (to_left, from_right, left_x))
        ):
            copy = pltpu.make_async_remote_copy(
                src_ref=source.at[:, there, :],
                dst_ref=target.at[:, there, :],
                send_sem=bulk_send.at[way, i],
                recv_sem=bulk_recv.at[way, i],
                device_id=(device, gy),
                device_id_type=MESH,
            )
            copy.start()
            sends.append(copy)

    for load in loads:
        load.wait()

    turn_pairs = jnp.where(owners_ref[...] == gx, lax.bitwise_and(dest_ref[...], 1), -1).astype(jnp.float32)
    turn_row = jnp.zeros((8, ROWS), jnp.float32)
    for j in range(2):
        pick = jnp.where(TILE * j + rows == 2 * lanes, 1.0, 0.0)
        turn_row += jnp.dot(
            jnp.broadcast_to(turn_pairs[j : j + 1], (8, TILE)), pick, preferred_element_type=jnp.float32
        )
    turn_row = turn_row[0:1]
    turn_b[...] = jnp.transpose(jnp.broadcast_to(turn_row, (ROWS, ROWS)))
    shift_row = shift_ref[...]
    shift_b[...] = jnp.transpose(jnp.broadcast_to(shift_row, (ROWS, ROWS)))


    filler = jnp.ones((G, TILE), jnp.float32)
    for ref in (zed, pl_x, pr_x, pl_y, pu_y):
        for half in range(2):
            ref[half, 0:G, :] = filler
            ref[half, ROWS + PAD : ROWS + PAD + G, :] = filler

    derive(15)
    over(0, 6, derive)
    over(1, 6, nodes)

    for half in range(2):
        for k, ref in enumerate((zed, pl_x, pr_x, pl_y)):
            outer_up[4 * half + k : 4 * half + k + 1, :] = ref[half, ROWS + PAD - 1 : ROWS + PAD, :]
        for k, ref in enumerate((zed, pl_x, pr_x, pu_y)):
            outer_down[4 * half + k : 4 * half + k + 1, :] = ref[half, PAD : PAD + 1, :]

    over(1, 5, cells)

    pl.semaphore_wait(barrier, 4)

    row_copies = []
    for way, (source, target, device) in enumerate(((outer_up, from_down, up_y), (outer_down, from_up, down_y))):
        copy = pltpu.make_async_remote_copy(
            src_ref=source, dst_ref=target, send_sem=row_send.at[way], recv_sem=row_recv.at[way],
            device_id=(gx, device), device_id_type=MESH,
        )
        copy.start()
        row_copies.append(copy)

    send_rows(0, 1, 4)
    for i, (first, last) in enumerate(RUNS[1:3]):
        top = min(last + 1, 15)
        over(first + 1, top, derive)
        over(first + 1, last + 1, nodes)
        over(first, last, cells)
        send_rows(1 + i, first, last - first)
    over(14, 15, derive)
    over(14, 16, nodes)
    over(13, 15, cells)

    packed_l = jnp.zeros((ROWS, TILE), jnp.float32)
    packed_r = jnp.zeros((ROWS, TILE), jnp.float32)
    for f, ref in enumerate((rho, ene, spx, spy, mat, lim)):
        first = ref[:, :TILE].astype(jnp.float32)
        last = ref[:, TILE:].astype(jnp.float32)
        inside = (lanes >= 4 * f) & (lanes < 4 * f + 4)
        packed_l = jnp.where(inside, pltpu.roll(first, 4 * f, 1) if f else first, packed_l)
        packed_r = jnp.where(inside, pltpu.roll(last, 4 * f + 4, 1), packed_r)
    seam_out_l[0:24, :] = jnp.transpose(packed_l)[0:24, :]
    seam_out_r[0:24, :] = jnp.transpose(packed_r)[0:24, :]

    for copy in row_copies:
        copy.wait()
    below = jnp.where(gy == 0, 0.0, from_down[...])
    above = jnp.where(gy == n_gy - 1, 0.0, from_up[...])
    for half in range(2):
        for k, ref in enumerate((zed, pl_x, pr_x, pl_y)):
            ref[half, PAD - 1 : PAD, :] = below[4 * half + k : 4 * half + k + 1, :]
        for k, ref in enumerate((zed, pl_x, pr_x, pu_y)):
            ref[half, ROWS + PAD : ROWS + PAD + 1, :] = above[4 * half + k : 4 * half + k + 1, :]
    outer_turned = jnp.transpose(
        jnp.concatenate([below, above, jnp.zeros((ROWS - 16, TILE), jnp.float32)], axis=0)
    )
    seam_out_l[24:32, :] = outer_turned[0:8, :]
    seam_out_r[24:32, :] = outer_turned[120:128, :]

    seam_copies = []
    for way, (source, target, device) in enumerate(
        ((seam_out_r, seam_in_l, right_x), (seam_out_l, seam_in_r, left_x))
    ):
        copy = pltpu.make_async_remote_copy(
            src_ref=source, dst_ref=target, send_sem=seam_send.at[way], recv_sem=seam_recv.at[way],
            device_id=(device, gy), device_id_type=MESH,
        )
        copy.start()
        seam_copies.append(copy)
    send_rows(3, 13, 2)
    nodes(0)
    nodes(16)
    cells(0)
    cells(15)
    send_rows(4, 0, 1)
    send_rows(5, 15, 1)

    for copy in seam_copies:
        copy.wait()

    sub8 = lax.broadcasted_iota(jnp.int32, (8, TILE), 0)
    lane8 = lax.broadcasted_iota(jnp.int32, (8, TILE), 1)

    def turned(x, by):
        return pltpu.roll(x, by % 8, 0) if by % 8 else x

    def seam_field(f):
        at, off = 8 * (f // 2), 4 * (f % 2)
        slots = []
        for before, after in ((seam_in_l, seam_out_l), (seam_out_r, seam_in_r)):
            head = turned(before[at : at + 8, :], 8 - off)
            tail = turned(after[at : at + 8, :], 4 - off + 8)
            slots.append(jnp.where(sub8 < 4, head, tail))
        return jnp.concatenate(slots, axis=0)

    def seam_outer(column):
        slots = []
        for before, after, b_off in ((seam_in_l, seam_out_l, 4), (seam_out_r, seam_in_r, 4)):
            head = turned(before[24:32, :], b_off)
            tail = turned(after[24:32, :], 4)
            slots.append(jnp.where(sub8 < 4, head, tail)[:, column : column + 1])
        return jnp.concatenate(slots, axis=0)

    density, energy, speed_x, speed_y, material, limiter = [seam_field(f) for f in range(6)]
    impedance, pressure = cell_state(density, energy, material)
    push_x = impedance * speed_x
    push_y = impedance * speed_y
    first_lane = lax.broadcasted_iota(jnp.int32, (16, ROWS), 1)
    at_first = first_lane == 0
    at_last = first_lane == ROWS - 1

    is_before = lax.broadcasted_iota(jnp.int32, (16, 1), 0)
    is_before = lax.rem(is_before, 8) < 4

    def outer_value(k):
        return jnp.where(is_before, seam_outer(4 + k), seam_outer(k))

    mine_l = (impedance, push_x + pressure, push_x - pressure, push_y + pressure)
    mine_u = (impedance, push_x + pressure, push_x - pressure, push_y - pressure)
    under = [jnp.where(at_first, outer_value(k), pltpu.roll(x, 1, 1)) for k, x in enumerate(mine_l)]
    over_it = [jnp.where(at_last, outer_value(8 + k), pltpu.roll(x, ROWS - 1, 1)) for k, x in enumerate(mine_u)]

    def seam_left(x):
        return pltpu.roll(x, 1, 0)

    def seam_right(x):
        return pltpu.roll(x, 15, 0)

    low = node_speed(under, mine_u, seam_left)
    high = node_speed(mine_l, over_it, seam_left)
    sub16 = lax.rem(lax.broadcasted_iota(jnp.int32, (16, ROWS), 0), 8)
    sums = remap_parts(
        density, energy, speed_x, speed_y, impedance, pressure, limiter, low + high,
        jnp.broadcast_to(shift_row, (16, ROWS)), (sub16 >= 2) & (sub16 < 6), seam_left, seam_right,
    )
    stay = turn_row == 0.0
    goes_right = turn_row == 1.0
    goes_left = turn_row == -1.0
    pieces = []
    for f in range(4):
        at_left, at_right = sums[f][0:8], sums[f][8:16]
        moved = jnp.where(goes_right, at_left, jnp.where(goes_left, at_right, 0.0))
        pieces.append(jnp.where(sub8 < 4, moved, jnp.where(stay, at_left, 0.0)))
        pieces.append(jnp.where(sub8 < 4, jnp.where(stay, at_right, 0.0), moved))
    rim[...] = jnp.transpose(jnp.concatenate(pieces + [jnp.zeros((64, ROWS), jnp.float32)], axis=0))

    near_edge = (lane8 < 3) | (lane8 >= TILE - 2)

    def prepare(g, carry):
        here = pl.ds(pl.multiple_of(g * G, G), G)
        turn = turn_b[here, :]
        edge = rim[here, :]
        for f in range(4):
            first, second = to_left[f, here, :], to_right[f, here, :]
            for half in range(2):
                q = 2 * f + half
                if half == 0:
                    value = jnp.where(turn == 0.0, first, jnp.where(turn == 1.0, 0.0, second))
                else:
                    value = jnp.where(turn == 0.0, second, jnp.where(turn == 1.0, first, 0.0))
                extra = pltpu.roll(edge, (2 * TILE - 8 * q - 4) % TILE, 1)
                out_ref[f, 0, here, half * TILE : (half + 1) * TILE] = value + jnp.where(near_edge, extra, 0.0)
        return carry

    def finish(g, carry=None):
        here = pl.ds(pl.multiple_of(g * G, G), G)
        turn = turn_b[here, :]
        for f in range(4):
            out_ref[f, 0, here, :TILE] += jnp.where(turn == 1.0, from_left[f, here, :], 0.0)
            out_ref[f, 0, here, TILE:] += jnp.where(turn == -1.0, from_right[f, here, :], 0.0)
        return carry

    over(0, 16, prepare)

    for i, (first, last) in enumerate(((1, 5), (5, 9), (9, 13), (13, 15), (0, 1), (15, 16))):
        sends[2 * i].wait()
        sends[2 * i + 1].wait()
        over(first, last, finish)


def on_device(n_gx, n_gy, density, velocity, energy, material, limiter, owners, dest_tile, tile_shift):
    dma = pltpu.SemaphoreType.DMA
    f32 = jnp.float32
    block = pltpu.VMEM((ROWS, COLS), f32)
    padded = pltpu.VMEM((2, ROWS + 2 * PAD, TILE), f32)
    tiles = pltpu.VMEM((4, ROWS, TILE), f32)
    square = pltpu.VMEM((ROWS, TILE), f32)
    small = pltpu.VMEM((8, TILE), f32)
    seam = pltpu.VMEM((32, ROWS), f32)
    any_space = pl.BlockSpec(memory_space=pltpu.HBM)
    vmem = pl.BlockSpec(memory_space=pltpu.VMEM)
    return pl.pallas_call(
        functools.partial(kernel, n_gx, n_gy),
        out_shape=pltpu.VMEM((4, 1, ROWS, COLS), f32),
        in_specs=[any_space] * 8,
        out_specs=vmem,
        scratch_shapes=[
            pltpu.VMEM((2, TILE), jnp.int32), pltpu.VMEM((2, TILE), jnp.int32), pltpu.VMEM((1, ROWS), f32),
            block, block, block, block,
            pltpu.VMEM((ROWS, COLS), jnp.int32), pltpu.VMEM((ROWS, COLS), jnp.int32),
            padded, block, padded, padded, padded, padded, padded, padded, square, square,
            tiles, tiles, tiles, tiles,
            small, small, small, small, seam, seam, seam, seam, square,
            dma((9,)), dma((2, 6)), dma((2, 6)), dma((2,)), dma((2,)), dma((2,)), dma((2,)),
        ],
        compiler_params=pltpu.CompilerParams(
            collective_id=0, has_side_effects=True, vmem_limit_bytes=58 * 1024 * 1024
        ),
    )(
        density, velocity, energy, material, limiter,
        owners.reshape(2, TILE), dest_tile.reshape(2, TILE), tile_shift,
    )


def solution(mesh):
    placed = (
        P(None, "gy", "gx"),
        P(None, None, "gy", "gx"),
        P(None, "gy", "gx"),
        P(None, "gy", "gx"),
        P(None, "gy", "gx"),
        P(("gx", "gy")),
        P(("gx", "gy")),
        P(None, "gy"),
    )
    return jax.shard_map(
        functools.partial(on_device, mesh.shape["gx"], mesh.shape["gy"]),
        mesh=mesh, in_specs=placed, out_specs=P(None, None, "gy", "gx"), check_vma=False,
    )
```

```python
import functools

import jax
import jax.numpy as jnp
from jax import lax
from jax.experimental import pallas as pl
from jax.experimental.pallas import tpu as pltpu
from jax.sharding import PartitionSpec as P

MESH = pl.DeviceIdType.MESH
TILE = 128
ROWS = 128
COLS = 256
PAD = 8
G = 8
time_step = 0.05

RUNS = ((1, 5), (5, 9), (9, 13), (13, 15))
EARLY = 6
DETOURS = {1: 2, 5: 2, 9: 2}
RELAY = 3


def by_material(material, first, second, third):
    return jnp.where(material == 0, first, jnp.where(material == 1, second, third))


def cell_state(density, energy, material):
    pressure = by_material(material, 0.4, 2.0 / 3.0, 2.0) * density * energy
    squared = by_material(material, 0.56, 10.0 / 9.0, 6.0) * energy
    return density * jnp.sqrt(squared), pressure


def node_speed(low, high, left):
    weight = low[0] + high[0]
    from_left = low[1] + high[1]
    from_right = low[2] + high[2]
    along_y = low[3] + high[3]
    scale = 1.0 / (left(weight) + weight)
    return (left(from_left) + from_right) * scale, (left(along_y) + along_y) * scale


def remap_parts(density, energy, speed_x, speed_y, impedance, pressure, limiter, nodes, shift, mask, left, right):
    low_x, low_y, high_x, high_y = nodes
    edge_x = low_x + high_x
    edge_y = low_y + high_y
    turn_y = high_y - low_y
    square = low_x * low_x + high_x * high_x + low_y * low_y + high_y * high_y
    next_x = right(edge_x)
    sum_x = edge_x + next_x
    sum_y = edge_y + right(edge_y)
    volume_rate = 0.5 * ((next_x - edge_x) + (turn_y + right(turn_y)))
    relaxation = (square + right(square)) - speed_x * sum_x - speed_y * sum_y
    half = 0.5 * impedance
    work = half * relaxation - pressure * volume_rate
    left_move = (0.5 * time_step) * edge_x
    right_move = (0.5 * time_step) * next_x
    scale = 1.0 / (1.0 + (right_move - left_move))
    total = density * (energy + 0.5 * (speed_x * speed_x + speed_y * speed_y))
    conserved = (
        density,
        density * speed_x + (time_step * half) * (sum_x - 4.0 * speed_x),
        density * speed_y + (time_step * half) * (sum_y - 4.0 * speed_y),
        total + time_step * work,
    )
    reach = jnp.where(limiter == 1, 2.0, 1.0)
    left_pos = shift + left_move
    right_pos = 1.0 + shift + right_move
    centre = 0.5 * (left_pos + right_pos)
    low_own = jnp.maximum(left_pos, 0.0)
    high_own = jnp.minimum(right_pos, 1.0)
    span_own = jnp.where(mask, jnp.maximum(high_own - low_own, 0.0), 0.0)
    offset_own = 0.5 * (high_own + low_own) - centre
    low_next = jnp.maximum(left_pos, 1.0)
    high_next = jnp.minimum(right_pos, 2.0)
    span_next = jnp.where(mask, jnp.maximum(high_next - low_next, 0.0), 0.0)
    offset_next = 0.5 * (high_next + low_next) - centre
    sums = []
    for field in conserved:
        value = field * scale
        back = value - left(value)
        fore = right(back)
        half_sum = 0.5 * (back + fore)
        limit = reach * jnp.minimum(jnp.abs(back), jnp.abs(fore))
        slope = jnp.where(back * fore > 0.0, jnp.maximum(jnp.minimum(half_sum, limit), -limit), 0.0)
        part_own = span_own * (value + slope * offset_own)
        part_next = span_next * (value + slope * offset_next)
        sums.append(part_own + left(part_next))
    return sums


def kernel(
    n_gx, n_gy,
    density_in, velocity_in, energy_in, material_in, limiter_in, owners_in, dest_in, shift_in, out_ref,
    owners_ref, dest_ref, shift_ref, rho, spx, spy, ene, mat, lim, zed, pre, pl_x, pr_x, pl_y, pu_y, node_x, node_y, shift_b, turn_b,
    to_left, to_right, from_left, from_right, outer, from_down, from_up, corner_ld, corner_lu, corner_rd, corner_ru,
    seam_out_l, seam_out_r, seam_in_l, seam_in_r, rim, passing,
    in_sem, bulk_send, bulk_recv, row_send, row_recv, corner_send, corner_recv, seam_send, seam_recv, relay_send, relay_recv,
):
    gx = lax.axis_index("gx")
    gy = lax.axis_index("gy")
    right_x = lax.rem(gx + 1, n_gx)
    left_x = lax.rem(gx + n_gx - 1, n_gx)
    up_y = lax.rem(gy + 1, n_gy)
    down_y = lax.rem(gy + n_gy - 1, n_gy)

    small_loads = [
        pltpu.make_async_copy(source, target, in_sem.at[0, 6 + k])
        for k, (source, target) in enumerate(((shift_in, shift_ref), (owners_in, owners_ref), (dest_in, dest_ref)))
    ]
    fields = (
        (density_in.at[0], rho),
        (energy_in.at[0], ene),
        (material_in.at[0], mat),
        (velocity_in.at[0, 0], spx),
        (velocity_in.at[1, 0], spy),
        (limiter_in.at[0], lim),
    )
    slabs = (pl.ds(0, EARLY * G), pl.ds(ROWS - G, G), pl.ds(EARLY * G, ROWS - G - EARLY * G))
    loads = [
        [pltpu.make_async_copy(source.at[part, :], target.at[part, :], in_sem.at[i, k]) for k, (source, target) in enumerate(fields)]
        for i, part in enumerate(slabs)
    ]
    for load in small_loads[:1] + loads[0] + loads[1] + loads[2] + small_loads[1:]:
        load.start()

    has_up = gy < n_gy - 1
    has_down = gy > 0
    barrier = pltpu.get_barrier_semaphore()

    def greet(column, level):
        pl.semaphore_signal(barrier, inc=1, device_id=(column, level), device_id_type=MESH)

    greet(left_x, gy)
    greet(right_x, gy)
    pl.when(has_up)(lambda: greet(gx, up_y))
    pl.when(has_down)(lambda: greet(gx, down_y))
    is_last = gx == n_gx - 1
    is_relay = gx == RELAY
    pl.when(is_relay)(lambda: greet(n_gx - 1, gy))

    @pl.when(gx == 0)
    def _():
        greet(RELAY, gy)
        pl.when(has_up)(lambda: greet(left_x, up_y))
        pl.when(has_down)(lambda: greet(left_x, down_y))


    lanes = lax.broadcasted_iota(jnp.int32, (ROWS, TILE), 1)
    rows = lax.broadcasted_iota(jnp.int32, (ROWS, TILE), 0)

    def wide(ref, start):
        return jnp.concatenate([ref[0, pl.ds(start, G), :], ref[1, pl.ds(start, G), :]], axis=1)

    def keep(ref, start, value):
        ref[0, pl.ds(start, G), :] = value[:, :TILE]
        ref[1, pl.ds(start, G), :] = value[:, TILE:]

    def left(x):
        return pltpu.roll(x, 1, 1)

    def right(x):
        return pltpu.roll(x, COLS - 1, 1)

    def derive(g, carry=None):
        at = pl.multiple_of(g * G, G)
        density = rho[pl.ds(at, G), :]
        speed_x = spx[pl.ds(at, G), :]
        speed_y = spy[pl.ds(at, G), :]
        impedance, pressure = cell_state(density, ene[pl.ds(at, G), :], mat[pl.ds(at, G), :])
        pad_at = pl.multiple_of(at + PAD, G)
        keep(zed, pad_at, impedance)
        pre[pl.ds(at, G), :] = pressure
        push_x = impedance * speed_x
        push_y = impedance * speed_y
        keep(pl_x, pad_at, push_x + pressure)
        keep(pr_x, pad_at, push_x - pressure)
        keep(pl_y, pad_at, push_y + pressure)
        keep(pu_y, pad_at, push_y - pressure)
        return carry

    def nodes(g, carry=None):
        at = pl.multiple_of(g * G, G)
        low = [wide(ref, at + PAD - 1) for ref in (zed, pl_x, pr_x, pl_y)]
        high = [wide(ref, pl.multiple_of(at + PAD, G)) for ref in (zed, pl_x, pr_x, pu_y)]
        x, y = node_speed(low, high, left)
        keep(node_x, at, x)
        keep(node_y, at, y)
        return carry

    inner = lax.broadcasted_iota(jnp.int32, (G, COLS), 1)
    inner = (inner >= 2) & (inner < COLS - 2)

    def cells(g, carry=None):
        at = pl.multiple_of(g * G, G)
        here = pl.ds(at, G)
        near = [wide(node_x, at), wide(node_y, at), wide(node_x, at + 1), wide(node_y, at + 1)]
        shift = shift_b[here, :]
        sums = remap_parts(
            rho[here, :], ene[here, :], spx[here, :], spy[here, :],
            wide(zed, pl.multiple_of(at + PAD, G)), pre[here, :], lim[here, :], near,
            jnp.concatenate([shift, shift], axis=1), inner, left, right,
        )
        for f in range(4):
            to_left[f, here, :] = sums[f][:, :TILE]
            to_right[f, here, :] = sums[f][:, TILE:]
        return carry

    def over(first, last, step):
        lax.fori_loop(first, last, step, None, unroll=min(4, last - first))

    def remote(source, target, send_sem, recv_sem, column, level=gy):
        return pltpu.make_async_remote_copy(
            src_ref=source, dst_ref=target, send_sem=send_sem, recv_sem=recv_sem,
            device_id=(column, level), device_id_type=MESH,
        )

    parts = []
    sends = []
    around, onward = [], []

    def send_part(first, last, detour=False):
        i = len(parts)
        parts.append((first, last))
        there = pl.ds(first * G, (last - first) * G)
        go_right = remote(
            to_right.at[:, there, :], from_left.at[:, there, :], bulk_send.at[0, i], bulk_recv.at[0, i], right_x
        )
        go_left = remote(
            to_left.at[:, there, :], from_right.at[:, there, :], bulk_send.at[1, i], bulk_recv.at[1, i], left_x
        )
        sends.extend((go_right, go_left))
        if detour:
            k = len(around)
            stop = passing.at[k, :, pl.ds(0, (last - first) * G), :]
            around.append(remote(to_right.at[:, there, :], stop, bulk_send.at[0, i], relay_recv.at[k], RELAY))
            onward.append(remote(stop, from_left.at[:, there, :], relay_send.at[k], bulk_recv.at[0, i], 0))
            pl.when(is_last)(lambda: around[k].start())
            pl.when(jnp.logical_not(is_last))(lambda: go_right.start())
        else:
            go_right.start()
        go_left.start()

    def send_run(first, last):
        extra = DETOURS.get(first, 0)
        if extra:
            send_part(first, first + extra, True)
        if first + extra < last:
            send_part(first + extra, last)

    filler = jnp.ones((G, TILE), jnp.float32)
    for ref in (zed, pl_x, pr_x, pl_y, pu_y):
        for half in range(2):
            ref[half, 0:G, :] = filler
            ref[half, ROWS + PAD : ROWS + PAD + G, :] = filler

    small_loads[0].wait()
    shift_row = shift_ref[...]
    shift_b[...] = jnp.transpose(jnp.broadcast_to(shift_row, (ROWS, ROWS)))

    for load in loads[0] + loads[1]:
        load.wait()
    derive(15)
    over(0, 6, derive)

    for half in range(2):
        for k, ref in enumerate((zed, pl_x, pr_x, pl_y)):
            outer[4 * half + k : 4 * half + k + 1, :] = ref[half, ROWS + PAD - 1 : ROWS + PAD, :]
        for k, ref in enumerate((zed, pl_x, pr_x, pu_y)):
            outer[8 + 4 * half + k : 8 + 4 * half + k + 1, :] = ref[half, PAD : PAD + 1, :]
    outer_turned = jnp.transpose(
        jnp.concatenate([outer[0:16, :], jnp.zeros((ROWS - 16, TILE), jnp.float32)], axis=0)
    )
    outer[16:24, :] = outer_turned[0:8, :]
    outer[24:32, :] = outer_turned[120:128, :]

    over(1, 6, nodes)
    over(1, 5, cells)


    beside_count = has_up.astype(jnp.int32) + has_down.astype(jnp.int32)
    met = 2 + beside_count + jnp.where(is_last | is_relay, 1, 0) + jnp.where(is_last, beside_count, 0)
    pl.semaphore_wait(barrier, met)

    row_copies = (
        remote(outer, from_down, row_send.at[0], row_recv.at[0], gx, up_y),
        remote(outer, from_up, row_send.at[1], row_recv.at[1], gx, down_y),
    )
    straight = (
        remote(outer.at[24:32, :], corner_ld, corner_send.at[0], corner_recv.at[0], right_x, up_y),
        remote(outer.at[24:32, :], corner_lu, corner_send.at[1], corner_recv.at[1], right_x, down_y),
    )

    def beside(copies, flags, act):
        for copy, flag in zip(copies, flags, strict=True):

            @pl.when(flag)
            def _(copy=copy):
                act(copy)

    def begin(copy):
        copy.start()

    def has_come(copy):
        copy.wait_recv()

    def has_gone(copy):
        copy.wait_send()

    beside(row_copies, (has_up, has_down), begin)
    pl.when(is_last)(lambda: beside(straight, (has_up, has_down), begin))

    send_part(1, 3, True)
    send_part(3, 5)
    for load in loads[2] + small_loads[1:]:
        load.wait()

    packed_l = jnp.zeros((ROWS, TILE), jnp.float32)
    packed_r = jnp.zeros((ROWS, TILE), jnp.float32)
    for f, ref in enumerate((rho, ene, spx, spy, mat, lim)):
        first = ref[:, :TILE].astype(jnp.float32)
        last = ref[:, TILE:].astype(jnp.float32)
        inside = (lanes >= 4 * f) & (lanes < 4 * f + 4)
        packed_l = jnp.where(inside, pltpu.roll(first, 4 * f, 1) if f else first, packed_l)
        packed_r = jnp.where(inside, pltpu.roll(last, 4 * f + 4, 1), packed_r)
    seam_out_l[...] = jnp.transpose(packed_l)[0:24, :]
    seam_out_r[...] = jnp.transpose(packed_r)[0:24, :]

    seam_copies = (
        remote(seam_out_r, seam_in_l, seam_send.at[0], seam_recv.at[0], right_x),
        remote(seam_out_l, seam_in_r, seam_send.at[1], seam_recv.at[1], left_x),
    )
    for copy in seam_copies:
        copy.start()

    for i, (first, last) in enumerate(RUNS[1:3]):
        top = min(last + 1, 15)
        over(first + 1, top, derive)
        over(first + 1, last + 1, nodes)
        over(first, last, cells)
        send_run(first, last)
    over(14, 15, derive)
    over(14, 16, nodes)
    over(13, 15, cells)
    send_run(13, 15)

    @pl.when(jnp.logical_not(has_down))
    def _():
        from_down[...] = jnp.zeros_like(from_down)
        corner_ld[...] = jnp.zeros_like(corner_ld)
        corner_rd[...] = jnp.zeros_like(corner_rd)

    @pl.when(jnp.logical_not(has_up))
    def _():
        from_up[...] = jnp.zeros_like(from_up)
        corner_lu[...] = jnp.zeros_like(corner_lu)
        corner_ru[...] = jnp.zeros_like(corner_ru)

    beside(row_copies, (has_down, has_up), has_come)
    onward_right = (
        remote(from_down.at[24:32, :], corner_ld, corner_send.at[0], corner_recv.at[0], right_x),
        remote(from_up.at[24:32, :], corner_lu, corner_send.at[1], corner_recv.at[1], right_x),
    )
    onward_left = (
        remote(from_down.at[16:24, :], corner_rd, corner_send.at[2], corner_recv.at[2], left_x),
        remote(from_up.at[16:24, :], corner_ru, corner_send.at[3], corner_recv.at[3], left_x),
    )
    pl.when(jnp.logical_not(is_last))(lambda: beside(onward_right, (has_down, has_up), begin))
    beside(onward_left, (has_down, has_up), begin)
    below = from_down[0:8, :]
    above = from_up[8:16, :]
    for half in range(2):
        for k, ref in enumerate((zed, pl_x, pr_x, pl_y)):
            ref[half, PAD - 1 : PAD, :] = below[4 * half + k : 4 * half + k + 1, :]
        for k, ref in enumerate((zed, pl_x, pr_x, pu_y)):
            ref[half, ROWS + PAD : ROWS + PAD + 1, :] = above[4 * half + k : 4 * half + k + 1, :]
    nodes(0)
    nodes(16)
    cells(0)
    cells(15)
    send_run(0, 1)
    send_run(15, 16)

    @pl.when(is_relay)
    def _():
        for arrival, departure in zip(around, onward, strict=True):
            arrival.wait_recv()
            departure.start()


    turn_pairs = jnp.where(owners_ref[...] == gx, lax.bitwise_and(dest_ref[...], 1), -1).astype(jnp.float32)
    turn_row = jnp.zeros((8, ROWS), jnp.float32)
    for j in range(2):
        pick = jnp.where(TILE * j + rows == 2 * lanes, 1.0, 0.0)
        turn_row += jnp.dot(
            jnp.broadcast_to(turn_pairs[j : j + 1], (8, TILE)), pick, preferred_element_type=jnp.float32
        )
    turn_row = turn_row[0:1]
    turn_b[...] = jnp.transpose(jnp.broadcast_to(turn_row, (ROWS, ROWS)))
    for copy in seam_copies:
        copy.wait_recv()
    beside(onward_right + onward_left, (has_down, has_up) * 2, has_come)

    sub8 = lax.broadcasted_iota(jnp.int32, (8, TILE), 0)
    lane8 = lax.broadcasted_iota(jnp.int32, (8, TILE), 1)

    def turned(x, by):
        return pltpu.roll(x, by % 8, 0) if by % 8 else x

    def seam_field(f):
        at, off = 8 * (f // 2), 4 * (f % 2)
        slots = []
        for before, after in ((seam_in_l, seam_out_l), (seam_out_r, seam_in_r)):
            head = turned(before[at : at + 8, :], 8 - off)
            tail = turned(after[at : at + 8, :], 4 - off + 8)
            slots.append(jnp.where(sub8 < 4, head, tail))
        return jnp.concatenate(slots, axis=0)

    def seam_outer(before_l, after_l, before_r, after_r, lane):
        slots = [
            jnp.where(sub8 < 4, turned(before[...], 4)[:, lane + 4 : lane + 5], turned(after[...], 4)[:, lane : lane + 1])
            for before, after in ((before_l, after_l), (before_r, after_r))
        ]
        return jnp.concatenate(slots, axis=0)

    density, energy, speed_x, speed_y, material, limiter = [seam_field(f) for f in range(6)]
    impedance, pressure = cell_state(density, energy, material)
    push_x = impedance * speed_x
    push_y = impedance * speed_y
    first_lane = lax.broadcasted_iota(jnp.int32, (16, ROWS), 1)
    at_first = first_lane == 0
    at_last = first_lane == ROWS - 1

    lower = (corner_ld, from_down.at[16:24, :], from_down.at[24:32, :], corner_rd)
    upper = (corner_lu, from_up.at[16:24, :], from_up.at[24:32, :], corner_ru)
    mine_l = (impedance, push_x + pressure, push_x - pressure, push_y + pressure)
    mine_u = (impedance, push_x + pressure, push_x - pressure, push_y - pressure)
    under = [jnp.where(at_first, seam_outer(*lower, k), pltpu.roll(x, 1, 1)) for k, x in enumerate(mine_l)]
    over_it = [
        jnp.where(at_last, seam_outer(*upper, 8 + k), pltpu.roll(x, ROWS - 1, 1)) for k, x in enumerate(mine_u)
    ]

    def seam_left(x):
        return pltpu.roll(x, 1, 0)

    def seam_right(x):
        return pltpu.roll(x, 15, 0)

    low = node_speed(under, mine_u, seam_left)
    high = node_speed(mine_l, over_it, seam_left)
    sub16 = lax.rem(lax.broadcasted_iota(jnp.int32, (16, ROWS), 0), 8)
    sums = remap_parts(
        density, energy, speed_x, speed_y, impedance, pressure, limiter, low + high,
        jnp.broadcast_to(shift_row, (16, ROWS)), (sub16 >= 2) & (sub16 < 6), seam_left, seam_right,
    )
    stay = turn_row == 0.0
    goes_right = turn_row == 1.0
    goes_left = turn_row == -1.0
    pieces = []
    for f in range(4):
        at_left, at_right = sums[f][0:8], sums[f][8:16]
        moved = jnp.where(goes_right, at_left, jnp.where(goes_left, at_right, 0.0))
        pieces.append(jnp.where(sub8 < 4, moved, jnp.where(stay, at_left, 0.0)))
        pieces.append(jnp.where(sub8 < 4, jnp.where(stay, at_right, 0.0), moved))
    rim[...] = jnp.transpose(jnp.concatenate(pieces + [jnp.zeros((64, ROWS), jnp.float32)], axis=0))

    near_edge = (lane8 < 3) | (lane8 >= TILE - 2)

    def prepare(g, carry):
        here = pl.ds(pl.multiple_of(g * G, G), G)
        turn = turn_b[here, :]
        edge = rim[here, :]
        for f in range(4):
            first, second = to_left[f, here, :], to_right[f, here, :]
            for half in range(2):
                q = 2 * f + half
                if half == 0:
                    value = jnp.where(turn == 0.0, first, jnp.where(turn == 1.0, 0.0, second))
                else:
                    value = jnp.where(turn == 0.0, second, jnp.where(turn == 1.0, first, 0.0))
                extra = pltpu.roll(edge, (2 * TILE - 8 * q - 4) % TILE, 1)
                out_ref[f, 0, here, half * TILE : (half + 1) * TILE] = value + jnp.where(near_edge, extra, 0.0)
        return carry

    def finish(g, carry=None):
        here = pl.ds(pl.multiple_of(g * G, G), G)
        turn = turn_b[here, :]
        for f in range(4):
            out_ref[f, 0, here, :TILE] += jnp.where(turn == 1.0, from_left[f, here, :], 0.0)
            out_ref[f, 0, here, TILE:] += jnp.where(turn == -1.0, from_right[f, here, :], 0.0)
        return carry

    over(0, 16, prepare)

    for i, (first, last) in enumerate(parts):
        sends[2 * i].wait_recv()
        sends[2 * i + 1].wait_recv()
        over(first, last, finish)

    beside(row_copies, (has_up, has_down), has_gone)
    beside(onward_left, (has_down, has_up), has_gone)
    pl.when(is_last)(lambda: beside(straight, (has_up, has_down), has_gone))
    pl.when(jnp.logical_not(is_last))(lambda: beside(onward_right, (has_down, has_up), has_gone))
    for copy in (*seam_copies, *sends):
        copy.wait_send()

    @pl.when(is_relay)
    def _():
        for departure in onward:
            departure.wait_send()


def on_device(n_gx, n_gy, density, velocity, energy, material, limiter, owners, dest_tile, tile_shift):
    dma = pltpu.SemaphoreType.DMA
    f32 = jnp.float32
    block = pltpu.VMEM((ROWS, COLS), f32)
    padded = pltpu.VMEM((2, ROWS + 2 * PAD, TILE), f32)
    tiles = pltpu.VMEM((4, ROWS, TILE), f32)
    square = pltpu.VMEM((ROWS, TILE), f32)
    small = pltpu.VMEM((8, TILE), f32)
    seam = pltpu.VMEM((24, ROWS), f32)
    outer = pltpu.VMEM((32, TILE), f32)
    any_space = pl.BlockSpec(memory_space=pltpu.HBM)
    vmem = pl.BlockSpec(memory_space=pltpu.VMEM)
    return pl.pallas_call(
        functools.partial(kernel, n_gx, n_gy),
        out_shape=pltpu.VMEM((4, 1, ROWS, COLS), f32),
        in_specs=[any_space] * 8,
        out_specs=vmem,
        scratch_shapes=[
            pltpu.VMEM((2, TILE), jnp.int32), pltpu.VMEM((2, TILE), jnp.int32), pltpu.VMEM((1, ROWS), f32),
            block, block, block, block,
            pltpu.VMEM((ROWS, COLS), jnp.int32), pltpu.VMEM((ROWS, COLS), jnp.int32),
            padded, block, padded, padded, padded, padded, padded, padded, square, square,
            tiles, tiles, tiles, tiles,
            outer, outer, outer, small, small, small, small, seam, seam, seam, seam, square, pltpu.VMEM((len(DETOURS), 4, 4 * G, TILE), f32),
            dma((3, 9)), dma((2, 10)), dma((2, 10)),
            dma((2,)), dma((2,)), dma((4,)), dma((4,)), dma((2,)), dma((2,)),
            dma((len(DETOURS),)), dma((len(DETOURS),)),
        ],
        compiler_params=pltpu.CompilerParams(
            collective_id=0, has_side_effects=True, vmem_limit_bytes=58 * 1024 * 1024
        ),
    )(
        density, velocity, energy, material, limiter,
        owners.reshape(2, TILE), dest_tile.reshape(2, TILE), tile_shift,
    )


def solution(mesh):
    placed = (
        P(None, "gy", "gx"),
        P(None, None, "gy", "gx"),
        P(None, "gy", "gx"),
        P(None, "gy", "gx"),
        P(None, "gy", "gx"),
        P(("gx", "gy")),
        P(("gx", "gy")),
        P(None, "gy"),
    )
    return jax.shard_map(
        functools.partial(on_device, mesh.shape["gx"], mesh.shape["gy"]),
        mesh=mesh, in_specs=placed, out_specs=P(None, None, "gy", "gx"), check_vma=False,
    )
```

```python
import functools

import jax
import jax.numpy as jnp
from jax import lax
from jax.experimental import pallas as pl
from jax.experimental.pallas import tpu as pltpu
from jax.sharding import PartitionSpec as P

MESH = pl.DeviceIdType.MESH
TILE = 128
ROWS = 128
COLS = 256
PAD = 8
G = 8
time_step = 0.05

RUNS = ((1, 5), (5, 9), (9, 13), (13, 15))
EARLY = 6
DETOURS = {1: 2, 5: 2, 9: 2}
RELAY = 3


def by_material(material, first, second, third):
    return jnp.where(material == 0, first, jnp.where(material == 1, second, third))


def cell_state(density, energy, material):
    pressure = by_material(material, 0.4, 2.0 / 3.0, 2.0) * density * energy
    squared = by_material(material, 0.56, 10.0 / 9.0, 6.0) * energy
    return density * jnp.sqrt(squared), pressure


def node_speed(low, high, left):
    weight = low[0] + high[0]
    from_left = low[1] + high[1]
    from_right = low[2] + high[2]
    along_y = low[3] + high[3]
    scale = 1.0 / (left(weight) + weight)
    return (left(from_left) + from_right) * scale, (left(along_y) + along_y) * scale


def remap_parts(density, energy, speed_x, speed_y, impedance, pressure, limiter, nodes, shift, mask, left, right):
    low_x, low_y, high_x, high_y = nodes
    edge_x = low_x + high_x
    edge_y = low_y + high_y
    turn_y = high_y - low_y
    square = low_x * low_x + high_x * high_x + low_y * low_y + high_y * high_y
    next_x = right(edge_x)
    sum_x = edge_x + next_x
    sum_y = edge_y + right(edge_y)
    volume_rate = 0.5 * ((next_x - edge_x) + (turn_y + right(turn_y)))
    relaxation = (square + right(square)) - speed_x * sum_x - speed_y * sum_y
    half = 0.5 * impedance
    work = half * relaxation - pressure * volume_rate
    left_move = (0.5 * time_step) * edge_x
    right_move = (0.5 * time_step) * next_x
    scale = 1.0 / (1.0 + (right_move - left_move))
    total = density * (energy + 0.5 * (speed_x * speed_x + speed_y * speed_y))
    conserved = (
        density,
        density * speed_x + (time_step * half) * (sum_x - 4.0 * speed_x),
        density * speed_y + (time_step * half) * (sum_y - 4.0 * speed_y),
        total + time_step * work,
    )
    reach = jnp.where(limiter == 1, 2.0, 1.0)
    left_pos = shift + left_move
    right_pos = 1.0 + shift + right_move
    centre = 0.5 * (left_pos + right_pos)
    low_own = jnp.maximum(left_pos, 0.0)
    high_own = jnp.minimum(right_pos, 1.0)
    span_own = jnp.where(mask, jnp.maximum(high_own - low_own, 0.0), 0.0)
    offset_own = 0.5 * (high_own + low_own) - centre
    low_next = jnp.maximum(left_pos, 1.0)
    high_next = jnp.minimum(right_pos, 2.0)
    span_next = jnp.where(mask, jnp.maximum(high_next - low_next, 0.0), 0.0)
    offset_next = 0.5 * (high_next + low_next) - centre
    sums = []
    for field in conserved:
        value = field * scale
        back = value - left(value)
        fore = right(back)
        half_sum = 0.5 * (back + fore)
        limit = reach * jnp.minimum(jnp.abs(back), jnp.abs(fore))
        slope = jnp.where(back * fore > 0.0, jnp.maximum(jnp.minimum(half_sum, limit), -limit), 0.0)
        part_own = span_own * (value + slope * offset_own)
        part_next = span_next * (value + slope * offset_next)
        sums.append(part_own + left(part_next))
    return sums


def kernel(
    n_gx, n_gy,
    density_in, velocity_in, energy_in, material_in, limiter_in, owners_in, dest_in, shift_in, out_ref,
    owners_ref, dest_ref, shift_ref, rho, spx, spy, ene, mat, lim, zed, pre, pl_x, pr_x, pl_y, pu_y, node_x, node_y, shift_b, turn_b,
    to_left, to_right, from_left, from_right, outer, from_down, from_up, corner_ld, corner_lu, corner_rd, corner_ru,
    seam_out_l, seam_out_r, seam_in_l, seam_in_r, rim, passing,
    in_sem, bulk_send, bulk_recv, row_send, row_recv, corner_send, corner_recv, seam_send, seam_recv, relay_send, relay_recv,
):
    gx = lax.axis_index("gx")
    gy = lax.axis_index("gy")
    right_x = lax.rem(gx + 1, n_gx)
    left_x = lax.rem(gx + n_gx - 1, n_gx)
    up_y = lax.rem(gy + 1, n_gy)
    down_y = lax.rem(gy + n_gy - 1, n_gy)

    small_loads = [
        pltpu.make_async_copy(source, target, in_sem.at[0, 6 + k])
        for k, (source, target) in enumerate(((shift_in, shift_ref), (owners_in, owners_ref), (dest_in, dest_ref)))
    ]
    fields = (
        (density_in.at[0], rho),
        (energy_in.at[0], ene),
        (material_in.at[0], mat),
        (velocity_in.at[0, 0], spx),
        (velocity_in.at[1, 0], spy),
        (limiter_in.at[0], lim),
    )
    slabs = (pl.ds(0, EARLY * G), pl.ds(ROWS - G, G), pl.ds(EARLY * G, ROWS - G - EARLY * G))
    loads = [
        [pltpu.make_async_copy(source.at[part, :], target.at[part, :], in_sem.at[i, k]) for k, (source, target) in enumerate(fields)]
        for i, part in enumerate(slabs)
    ]
    for load in small_loads[:1] + loads[0] + loads[1] + loads[2] + small_loads[1:]:
        load.start()

    has_up = gy < n_gy - 1
    has_down = gy > 0
    barrier = pltpu.get_barrier_semaphore()

    def greet(column, level):
        pl.semaphore_signal(barrier, inc=1, device_id=(column, level), device_id_type=MESH)

    greet(left_x, gy)
    greet(right_x, gy)
    pl.when(has_up)(lambda: greet(gx, up_y))
    pl.when(has_down)(lambda: greet(gx, down_y))
    is_last = gx == n_gx - 1
    is_relay = gx == RELAY
    pl.when(is_relay)(lambda: greet(n_gx - 1, gy))

    @pl.when(gx == 0)
    def _():
        greet(RELAY, gy)
        pl.when(has_up)(lambda: greet(left_x, up_y))
        pl.when(has_down)(lambda: greet(left_x, down_y))


    lanes = lax.broadcasted_iota(jnp.int32, (ROWS, TILE), 1)
    rows = lax.broadcasted_iota(jnp.int32, (ROWS, TILE), 0)

    def wide(ref, start):
        return jnp.concatenate([ref[0, pl.ds(start, G), :], ref[1, pl.ds(start, G), :]], axis=1)

    def keep(ref, start, value):
        ref[0, pl.ds(start, G), :] = value[:, :TILE]
        ref[1, pl.ds(start, G), :] = value[:, TILE:]

    def left(x):
        return pltpu.roll(x, 1, 1)

    def right(x):
        return pltpu.roll(x, COLS - 1, 1)

    def derive(g, carry=None):
        at = pl.multiple_of(g * G, G)
        density = rho[pl.ds(at, G), :]
        speed_x = spx[pl.ds(at, G), :]
        speed_y = spy[pl.ds(at, G), :]
        impedance, pressure = cell_state(density, ene[pl.ds(at, G), :], mat[pl.ds(at, G), :])
        pad_at = pl.multiple_of(at + PAD, G)
        keep(zed, pad_at, impedance)
        pre[pl.ds(at, G), :] = pressure
        push_x = impedance * speed_x
        push_y = impedance * speed_y
        keep(pl_x, pad_at, push_x + pressure)
        keep(pr_x, pad_at, push_x - pressure)
        keep(pl_y, pad_at, push_y + pressure)
        keep(pu_y, pad_at, push_y - pressure)
        return carry

    def nodes(g, carry=None):
        at = pl.multiple_of(g * G, G)
        low = [wide(ref, at + PAD - 1) for ref in (zed, pl_x, pr_x, pl_y)]
        high = [wide(ref, pl.multiple_of(at + PAD, G)) for ref in (zed, pl_x, pr_x, pu_y)]
        x, y = node_speed(low, high, left)
        keep(node_x, at, x)
        keep(node_y, at, y)
        return carry

    inner = lax.broadcasted_iota(jnp.int32, (G, COLS), 1)
    inner = (inner >= 2) & (inner < COLS - 2)

    def cells(g, carry=None):
        at = pl.multiple_of(g * G, G)
        here = pl.ds(at, G)
        near = [wide(node_x, at), wide(node_y, at), wide(node_x, at + 1), wide(node_y, at + 1)]
        shift = shift_b[here, :]
        sums = remap_parts(
            rho[here, :], ene[here, :], spx[here, :], spy[here, :],
            wide(zed, pl.multiple_of(at + PAD, G)), pre[here, :], lim[here, :], near,
            jnp.concatenate([shift, shift], axis=1), inner, left, right,
        )
        for f in range(4):
            to_left[g, f] = sums[f][:, :TILE]
            to_right[g, f] = sums[f][:, TILE:]
        return carry

    def over(first, last, step):
        lax.fori_loop(first, last, step, None, unroll=min(4, last - first))

    def remote(source, target, send_sem, recv_sem, column, level=gy):
        return pltpu.make_async_remote_copy(
            src_ref=source, dst_ref=target, send_sem=send_sem, recv_sem=recv_sem,
            device_id=(column, level), device_id_type=MESH,
        )

    parts = []
    sends = []
    around, onward = [], []

    def send_part(first, last, detour=False):
        i = len(parts)
        parts.append((first, last))
        there = pl.ds(first, last - first)
        go_right = remote(
            to_right.at[there], from_left.at[there], bulk_send.at[0, i], bulk_recv.at[0, i], right_x
        )
        go_left = remote(
            to_left.at[there], from_right.at[there], bulk_send.at[1, i], bulk_recv.at[1, i], left_x
        )
        sends.extend((go_right, go_left))
        if detour:
            k = len(around)
            stop = passing.at[k, pl.ds(0, last - first)]
            around.append(remote(to_right.at[there], stop, bulk_send.at[0, i], relay_recv.at[k], RELAY))
            onward.append(remote(stop, from_left.at[there], relay_send.at[k], bulk_recv.at[0, i], 0))
            pl.when(is_last)(lambda: around[k].start())
            pl.when(jnp.logical_not(is_last))(lambda: go_right.start())
        else:
            go_right.start()
        go_left.start()

    def send_run(first, last):
        extra = DETOURS.get(first, 0)
        if extra:
            send_part(first, first + extra, True)
        if first + extra < last:
            send_part(first + extra, last)

    filler = jnp.ones((G, TILE), jnp.float32)
    for ref in (zed, pl_x, pr_x, pl_y, pu_y):
        for half in range(2):
            ref[half, 0:G, :] = filler
            ref[half, ROWS + PAD : ROWS + PAD + G, :] = filler

    small_loads[0].wait()
    shift_row = shift_ref[...]
    shift_b[...] = jnp.transpose(jnp.broadcast_to(shift_row, (ROWS, ROWS)))

    for load in loads[0] + loads[1]:
        load.wait()
    derive(15)
    over(0, 6, derive)

    for half in range(2):
        for k, ref in enumerate((zed, pl_x, pr_x, pl_y)):
            outer[4 * half + k : 4 * half + k + 1, :] = ref[half, ROWS + PAD - 1 : ROWS + PAD, :]
        for k, ref in enumerate((zed, pl_x, pr_x, pu_y)):
            outer[8 + 4 * half + k : 8 + 4 * half + k + 1, :] = ref[half, PAD : PAD + 1, :]
    outer_turned = jnp.transpose(
        jnp.concatenate([outer[0:16, :], jnp.zeros((ROWS - 16, TILE), jnp.float32)], axis=0)
    )
    outer[16:24, :] = outer_turned[0:8, :]
    outer[24:32, :] = outer_turned[120:128, :]

    over(1, 6, nodes)
    over(1, 5, cells)


    beside_count = has_up.astype(jnp.int32) + has_down.astype(jnp.int32)
    met = 2 + beside_count + jnp.where(is_last | is_relay, 1, 0) + jnp.where(is_last, beside_count, 0)
    pl.semaphore_wait(barrier, met)

    row_copies = (
        remote(outer, from_down, row_send.at[0], row_recv.at[0], gx, up_y),
        remote(outer, from_up, row_send.at[1], row_recv.at[1], gx, down_y),
    )
    straight = (
        remote(outer.at[24:32, :], corner_ld, corner_send.at[0], corner_recv.at[0], right_x, up_y),
        remote(outer.at[24:32, :], corner_lu, corner_send.at[1], corner_recv.at[1], right_x, down_y),
    )

    def beside(copies, flags, act):
        for copy, flag in zip(copies, flags, strict=True):

            @pl.when(flag)
            def _(copy=copy):
                act(copy)

    def begin(copy):
        copy.start()

    def has_come(copy):
        copy.wait_recv()

    def has_gone(copy):
        copy.wait_send()

    beside(row_copies, (has_up, has_down), begin)
    pl.when(is_last)(lambda: beside(straight, (has_up, has_down), begin))

    send_part(1, 3, True)
    send_part(3, 5)
    for load in loads[2] + small_loads[1:]:
        load.wait()

    packed_l = jnp.zeros((ROWS, TILE), jnp.float32)
    packed_r = jnp.zeros((ROWS, TILE), jnp.float32)
    for f, ref in enumerate((rho, ene, spx, spy, mat, lim)):
        first = ref[:, :TILE].astype(jnp.float32)
        last = ref[:, TILE:].astype(jnp.float32)
        inside = (lanes >= 4 * f) & (lanes < 4 * f + 4)
        packed_l = jnp.where(inside, pltpu.roll(first, 4 * f, 1) if f else first, packed_l)
        packed_r = jnp.where(inside, pltpu.roll(last, 4 * f + 4, 1), packed_r)
    seam_out_l[...] = jnp.transpose(packed_l)[0:24, :]
    seam_out_r[...] = jnp.transpose(packed_r)[0:24, :]

    seam_copies = (
        remote(seam_out_r, seam_in_l, seam_send.at[0], seam_recv.at[0], right_x),
        remote(seam_out_l, seam_in_r, seam_send.at[1], seam_recv.at[1], left_x),
    )
    for copy in seam_copies:
        copy.start()

    for i, (first, last) in enumerate(RUNS[1:3]):
        top = min(last + 1, 15)
        over(first + 1, top, derive)
        over(first + 1, last + 1, nodes)
        over(first, last, cells)
        send_run(first, last)
    over(14, 15, derive)
    over(14, 16, nodes)
    over(13, 15, cells)
    send_run(13, 15)

    @pl.when(jnp.logical_not(has_down))
    def _():
        from_down[...] = jnp.zeros_like(from_down)
        corner_ld[...] = jnp.zeros_like(corner_ld)
        corner_rd[...] = jnp.zeros_like(corner_rd)

    @pl.when(jnp.logical_not(has_up))
    def _():
        from_up[...] = jnp.zeros_like(from_up)
        corner_lu[...] = jnp.zeros_like(corner_lu)
        corner_ru[...] = jnp.zeros_like(corner_ru)

    beside(row_copies, (has_down, has_up), has_come)
    onward_right = (
        remote(from_down.at[24:32, :], corner_ld, corner_send.at[0], corner_recv.at[0], right_x),
        remote(from_up.at[24:32, :], corner_lu, corner_send.at[1], corner_recv.at[1], right_x),
    )
    onward_left = (
        remote(from_down.at[16:24, :], corner_rd, corner_send.at[2], corner_recv.at[2], left_x),
        remote(from_up.at[16:24, :], corner_ru, corner_send.at[3], corner_recv.at[3], left_x),
    )
    pl.when(jnp.logical_not(is_last))(lambda: beside(onward_right, (has_down, has_up), begin))
    beside(onward_left, (has_down, has_up), begin)
    below = from_down[0:8, :]
    above = from_up[8:16, :]
    for half in range(2):
        for k, ref in enumerate((zed, pl_x, pr_x, pl_y)):
            ref[half, PAD - 1 : PAD, :] = below[4 * half + k : 4 * half + k + 1, :]
        for k, ref in enumerate((zed, pl_x, pr_x, pu_y)):
            ref[half, ROWS + PAD : ROWS + PAD + 1, :] = above[4 * half + k : 4 * half + k + 1, :]
    nodes(0)
    nodes(16)
    cells(0)
    cells(15)
    send_run(0, 1)
    send_run(15, 16)

    @pl.when(is_relay)
    def _():
        for arrival, departure in zip(around, onward, strict=True):
            arrival.wait_recv()
            departure.start()


    turn_pairs = jnp.where(owners_ref[...] == gx, lax.bitwise_and(dest_ref[...], 1), -1).astype(jnp.float32)
    turn_row = jnp.zeros((8, ROWS), jnp.float32)
    for j in range(2):
        pick = jnp.where(TILE * j + rows == 2 * lanes, 1.0, 0.0)
        turn_row += jnp.dot(
            jnp.broadcast_to(turn_pairs[j : j + 1], (8, TILE)), pick, preferred_element_type=jnp.float32
        )
    turn_row = turn_row[0:1]
    turn_b[...] = jnp.transpose(jnp.broadcast_to(turn_row, (ROWS, ROWS)))
    for copy in seam_copies:
        copy.wait_recv()
    beside(onward_right + onward_left, (has_down, has_up) * 2, has_come)

    sub8 = lax.broadcasted_iota(jnp.int32, (8, TILE), 0)
    lane8 = lax.broadcasted_iota(jnp.int32, (8, TILE), 1)

    def turned(x, by):
        return pltpu.roll(x, by % 8, 0) if by % 8 else x

    def seam_field(f):
        at, off = 8 * (f // 2), 4 * (f % 2)
        slots = []
        for before, after in ((seam_in_l, seam_out_l), (seam_out_r, seam_in_r)):
            head = turned(before[at : at + 8, :], 8 - off)
            tail = turned(after[at : at + 8, :], 4 - off + 8)
            slots.append(jnp.where(sub8 < 4, head, tail))
        return jnp.concatenate(slots, axis=0)

    def seam_outer(before_l, after_l, before_r, after_r, lane):
        slots = [
            jnp.where(sub8 < 4, turned(before[...], 4)[:, lane + 4 : lane + 5], turned(after[...], 4)[:, lane : lane + 1])
            for before, after in ((before_l, after_l), (before_r, after_r))
        ]
        return jnp.concatenate(slots, axis=0)

    density, energy, speed_x, speed_y, material, limiter = [seam_field(f) for f in range(6)]
    impedance, pressure = cell_state(density, energy, material)
    push_x = impedance * speed_x
    push_y = impedance * speed_y
    first_lane = lax.broadcasted_iota(jnp.int32, (16, ROWS), 1)
    at_first = first_lane == 0
    at_last = first_lane == ROWS - 1

    lower = (corner_ld, from_down.at[16:24, :], from_down.at[24:32, :], corner_rd)
    upper = (corner_lu, from_up.at[16:24, :], from_up.at[24:32, :], corner_ru)
    mine_l = (impedance, push_x + pressure, push_x - pressure, push_y + pressure)
    mine_u = (impedance, push_x + pressure, push_x - pressure, push_y - pressure)
    under = [jnp.where(at_first, seam_outer(*lower, k), pltpu.roll(x, 1, 1)) for k, x in enumerate(mine_l)]
    over_it = [
        jnp.where(at_last, seam_outer(*upper, 8 + k), pltpu.roll(x, ROWS - 1, 1)) for k, x in enumerate(mine_u)
    ]

    def seam_left(x):
        return pltpu.roll(x, 1, 0)

    def seam_right(x):
        return pltpu.roll(x, 15, 0)

    low = node_speed(under, mine_u, seam_left)
    high = node_speed(mine_l, over_it, seam_left)
    sub16 = lax.rem(lax.broadcasted_iota(jnp.int32, (16, ROWS), 0), 8)
    sums = remap_parts(
        density, energy, speed_x, speed_y, impedance, pressure, limiter, low + high,
        jnp.broadcast_to(shift_row, (16, ROWS)), (sub16 >= 2) & (sub16 < 6), seam_left, seam_right,
    )
    stay = turn_row == 0.0
    goes_right = turn_row == 1.0
    goes_left = turn_row == -1.0
    pieces = []
    for f in range(4):
        at_left, at_right = sums[f][0:8], sums[f][8:16]
        moved = jnp.where(goes_right, at_left, jnp.where(goes_left, at_right, 0.0))
        pieces.append(jnp.where(sub8 < 4, moved, jnp.where(stay, at_left, 0.0)))
        pieces.append(jnp.where(sub8 < 4, jnp.where(stay, at_right, 0.0), moved))
    rim[...] = jnp.transpose(jnp.concatenate(pieces + [jnp.zeros((64, ROWS), jnp.float32)], axis=0))

    near_edge = (lane8 < 3) | (lane8 >= TILE - 2)

    def prepare(g, carry):
        here = pl.ds(pl.multiple_of(g * G, G), G)
        turn = turn_b[here, :]
        edge = rim[here, :]
        for f in range(4):
            first, second = to_left[g, f], to_right[g, f]
            for half in range(2):
                q = 2 * f + half
                if half == 0:
                    value = jnp.where(turn == 0.0, first, jnp.where(turn == 1.0, 0.0, second))
                else:
                    value = jnp.where(turn == 0.0, second, jnp.where(turn == 1.0, first, 0.0))
                extra = pltpu.roll(edge, (2 * TILE - 8 * q - 4) % TILE, 1)
                out_ref[f, 0, here, half * TILE : (half + 1) * TILE] = value + jnp.where(near_edge, extra, 0.0)
        return carry

    def finish(g, carry=None):
        here = pl.ds(pl.multiple_of(g * G, G), G)
        turn = turn_b[here, :]
        for f in range(4):
            out_ref[f, 0, here, :TILE] += jnp.where(turn == 1.0, from_left[g, f], 0.0)
            out_ref[f, 0, here, TILE:] += jnp.where(turn == -1.0, from_right[g, f], 0.0)
        return carry

    over(0, 16, prepare)

    for i, (first, last) in enumerate(parts):
        sends[2 * i].wait_recv()
        sends[2 * i + 1].wait_recv()
        over(first, last, finish)

    beside(row_copies, (has_up, has_down), has_gone)
    beside(onward_left, (has_down, has_up), has_gone)
    pl.when(is_last)(lambda: beside(straight, (has_up, has_down), has_gone))
    pl.when(jnp.logical_not(is_last))(lambda: beside(onward_right, (has_down, has_up), has_gone))
    for copy in (*seam_copies, *sends):
        copy.wait_send()

    @pl.when(is_relay)
    def _():
        for departure in onward:
            departure.wait_send()


def on_device(n_gx, n_gy, density, velocity, energy, material, limiter, owners, dest_tile, tile_shift):
    dma = pltpu.SemaphoreType.DMA
    f32 = jnp.float32
    block = pltpu.VMEM((ROWS, COLS), f32)
    padded = pltpu.VMEM((2, ROWS + 2 * PAD, TILE), f32)
    tiles = pltpu.VMEM((ROWS // G, 4, G, TILE), f32)
    square = pltpu.VMEM((ROWS, TILE), f32)
    small = pltpu.VMEM((8, TILE), f32)
    seam = pltpu.VMEM((24, ROWS), f32)
    outer = pltpu.VMEM((32, TILE), f32)
    any_space = pl.BlockSpec(memory_space=pltpu.HBM)
    vmem = pl.BlockSpec(memory_space=pltpu.VMEM)
    return pl.pallas_call(
        functools.partial(kernel, n_gx, n_gy),
        out_shape=pltpu.VMEM((4, 1, ROWS, COLS), f32),
        in_specs=[any_space] * 8,
        out_specs=vmem,
        scratch_shapes=[
            pltpu.VMEM((2, TILE), jnp.int32), pltpu.VMEM((2, TILE), jnp.int32), pltpu.VMEM((1, ROWS), f32),
            block, block, block, block,
            pltpu.VMEM((ROWS, COLS), jnp.int32), pltpu.VMEM((ROWS, COLS), jnp.int32),
            padded, block, padded, padded, padded, padded, padded, padded, square, square,
            tiles, tiles, tiles, tiles,
            outer, outer, outer, small, small, small, small, seam, seam, seam, seam, square, pltpu.VMEM((len(DETOURS), 4, 4, G, TILE), f32),
            dma((3, 9)), dma((2, 10)), dma((2, 10)),
            dma((2,)), dma((2,)), dma((4,)), dma((4,)), dma((2,)), dma((2,)),
            dma((len(DETOURS),)), dma((len(DETOURS),)),
        ],
        compiler_params=pltpu.CompilerParams(
            collective_id=0, has_side_effects=True, vmem_limit_bytes=58 * 1024 * 1024
        ),
    )(
        density, velocity, energy, material, limiter,
        owners.reshape(2, TILE), dest_tile.reshape(2, TILE), tile_shift,
    )


def solution(mesh):
    placed = (
        P(None, "gy", "gx"),
        P(None, None, "gy", "gx"),
        P(None, "gy", "gx"),
        P(None, "gy", "gx"),
        P(None, "gy", "gx"),
        P(("gx", "gy")),
        P(("gx", "gy")),
        P(None, "gy"),
    )
    return jax.shard_map(
        functools.partial(on_device, mesh.shape["gx"], mesh.shape["gy"]),
        mesh=mesh, in_specs=placed, out_specs=P(None, None, "gy", "gx"), check_vma=False,
    )
```

```python
import functools

import jax
import jax.numpy as jnp
from jax import lax
from jax.experimental import pallas as pl
from jax.experimental.pallas import tpu as pltpu
from jax.sharding import PartitionSpec as P

MESH = pl.DeviceIdType.MESH
TILE = 128
ROWS = 128
COLS = 256
PAD = 8
G = 8
time_step = 0.05

RUNS = ((1, 5), (5, 9), (9, 13), (13, 15))
EARLY = 6
DETOURS = {1: 2, 5: 2, 9: 2}
RELAY = 3


def by_material(material, first, second, third):
    return jnp.where(material == 0, first, jnp.where(material == 1, second, third))


def cell_state(density, energy, material):
    pressure = by_material(material, 0.4, 2.0 / 3.0, 2.0) * density * energy
    squared = by_material(material, 0.56, 10.0 / 9.0, 6.0) * energy
    return density * jnp.sqrt(squared), pressure


def node_speed(low, high, left):
    weight = low[0] + high[0]
    from_left = low[1] + high[1]
    from_right = low[2] + high[2]
    along_y = low[3] + high[3]
    scale = 1.0 / (left(weight) + weight)
    return (left(from_left) + from_right) * scale, (left(along_y) + along_y) * scale


def remap_parts(density, energy, speed_x, speed_y, impedance, pressure, limiter, nodes, shift, mask, left, right):
    low_x, low_y, high_x, high_y = nodes
    edge_x = low_x + high_x
    edge_y = low_y + high_y
    turn_y = high_y - low_y
    square = low_x * low_x + high_x * high_x + low_y * low_y + high_y * high_y
    next_x = right(edge_x)
    sum_x = edge_x + next_x
    sum_y = edge_y + right(edge_y)
    volume_rate = 0.5 * ((next_x - edge_x) + (turn_y + right(turn_y)))
    relaxation = (square + right(square)) - speed_x * sum_x - speed_y * sum_y
    half = 0.5 * impedance
    work = half * relaxation - pressure * volume_rate
    left_move = (0.5 * time_step) * edge_x
    right_move = (0.5 * time_step) * next_x
    scale = 1.0 / (1.0 + (right_move - left_move))
    total = density * (energy + 0.5 * (speed_x * speed_x + speed_y * speed_y))
    conserved = (
        density,
        density * speed_x + (time_step * half) * (sum_x - 4.0 * speed_x),
        density * speed_y + (time_step * half) * (sum_y - 4.0 * speed_y),
        total + time_step * work,
    )
    reach = jnp.where(limiter == 1, 2.0, 1.0)
    left_pos = shift + left_move
    right_pos = 1.0 + shift + right_move
    centre = 0.5 * (left_pos + right_pos)
    low_own = jnp.maximum(left_pos, 0.0)
    high_own = jnp.minimum(right_pos, 1.0)
    span_own = jnp.where(mask, jnp.maximum(high_own - low_own, 0.0), 0.0)
    offset_own = 0.5 * (high_own + low_own) - centre
    low_next = jnp.maximum(left_pos, 1.0)
    high_next = jnp.minimum(right_pos, 2.0)
    span_next = jnp.where(mask, jnp.maximum(high_next - low_next, 0.0), 0.0)
    offset_next = 0.5 * (high_next + low_next) - centre
    sums = []
    for field in conserved:
        value = field * scale
        back = value - left(value)
        fore = right(back)
        half_sum = 0.5 * (back + fore)
        limit = reach * jnp.minimum(jnp.abs(back), jnp.abs(fore))
        slope = jnp.where(back * fore > 0.0, jnp.maximum(jnp.minimum(half_sum, limit), -limit), 0.0)
        part_own = span_own * (value + slope * offset_own)
        part_next = span_next * (value + slope * offset_next)
        sums.append(part_own + left(part_next))
    return sums


def kernel(
    n_gx, n_gy,
    density_in, velocity_in, energy_in, material_in, limiter_in, owners_in, dest_in, shift_in, out_ref,
    owners_ref, dest_ref, shift_ref, rho, spx, spy, ene, mat, lim, zed, pre, pl_x, pr_x, pl_y, pu_y, node_x, node_y, shift_b, turn_b,
    to_left, to_right, from_left, from_right, outer, from_down, from_up, corner_ld, corner_lu, corner_rd, corner_ru,
    seam_out_l, seam_out_r, seam_in_l, seam_in_r, rim, passing,
    in_sem, bulk_send, bulk_recv, row_send, row_recv, corner_send, corner_recv, seam_send, seam_recv, relay_send, relay_recv,
):
    gx = lax.axis_index("gx")
    gy = lax.axis_index("gy")
    right_x = lax.rem(gx + 1, n_gx)
    left_x = lax.rem(gx + n_gx - 1, n_gx)
    up_y = lax.rem(gy + 1, n_gy)
    down_y = lax.rem(gy + n_gy - 1, n_gy)

    small_loads = [
        pltpu.make_async_copy(source, target, in_sem.at[0, 6 + k])
        for k, (source, target) in enumerate(((shift_in, shift_ref), (owners_in, owners_ref), (dest_in, dest_ref)))
    ]
    fields = (
        (density_in.at[0], rho),
        (energy_in.at[0], ene),
        (material_in.at[0], mat),
        (velocity_in.at[0, 0], spx),
        (velocity_in.at[1, 0], spy),
        (limiter_in.at[0], lim),
    )
    slabs = (pl.ds(0, EARLY * G), pl.ds(ROWS - G, G), pl.ds(EARLY * G, ROWS - G - EARLY * G))
    loads = [
        [pltpu.make_async_copy(source.at[part, :], target.at[part, :], in_sem.at[i, k]) for k, (source, target) in enumerate(fields)]
        for i, part in enumerate(slabs)
    ]
    for load in small_loads[:1] + loads[0] + loads[1] + loads[2] + small_loads[1:]:
        load.start()

    has_up = gy < n_gy - 1
    has_down = gy > 0
    barrier = pltpu.get_barrier_semaphore()

    def greet(column, level):
        pl.semaphore_signal(barrier, inc=1, device_id=(column, level), device_id_type=MESH)

    greet(left_x, gy)
    greet(right_x, gy)
    pl.when(has_up)(lambda: greet(gx, up_y))
    pl.when(has_down)(lambda: greet(gx, down_y))
    is_last = gx == n_gx - 1
    is_relay = gx == RELAY
    pl.when(is_relay)(lambda: greet(n_gx - 1, gy))

    @pl.when(gx == 0)
    def _():
        greet(RELAY, gy)
        pl.when(has_up)(lambda: greet(left_x, up_y))
        pl.when(has_down)(lambda: greet(left_x, down_y))


    lanes = lax.broadcasted_iota(jnp.int32, (ROWS, TILE), 1)
    rows = lax.broadcasted_iota(jnp.int32, (ROWS, TILE), 0)

    def wide(ref, start):
        return jnp.concatenate([ref[0, pl.ds(start, G), :], ref[1, pl.ds(start, G), :]], axis=1)

    def keep(ref, start, value):
        ref[0, pl.ds(start, G), :] = value[:, :TILE]
        ref[1, pl.ds(start, G), :] = value[:, TILE:]

    def left(x):
        return pltpu.roll(x, 1, 1)

    def right(x):
        return pltpu.roll(x, COLS - 1, 1)

    def derive(g, carry=None):
        at = pl.multiple_of(g * G, G)
        density = rho[pl.ds(at, G), :]
        speed_x = spx[pl.ds(at, G), :]
        speed_y = spy[pl.ds(at, G), :]
        impedance, pressure = cell_state(density, ene[pl.ds(at, G), :], mat[pl.ds(at, G), :])
        pad_at = pl.multiple_of(at + PAD, G)
        keep(zed, pad_at, impedance)
        pre[pl.ds(at, G), :] = pressure
        push_x = impedance * speed_x
        push_y = impedance * speed_y
        keep(pl_x, pad_at, push_x + pressure)
        keep(pr_x, pad_at, push_x - pressure)
        keep(pl_y, pad_at, push_y + pressure)
        keep(pu_y, pad_at, push_y - pressure)
        return carry

    def nodes(g, carry=None):
        at = pl.multiple_of(g * G, G)
        low = [wide(ref, at + PAD - 1) for ref in (zed, pl_x, pr_x, pl_y)]
        high = [wide(ref, pl.multiple_of(at + PAD, G)) for ref in (zed, pl_x, pr_x, pu_y)]
        x, y = node_speed(low, high, left)
        keep(node_x, at, x)
        keep(node_y, at, y)
        return carry

    inner = lax.broadcasted_iota(jnp.int32, (G, COLS), 1)
    inner = (inner >= 2) & (inner < COLS - 2)

    def cells(g, carry=None):
        at = pl.multiple_of(g * G, G)
        here = pl.ds(at, G)
        near = [wide(node_x, at), wide(node_y, at), wide(node_x, at + 1), wide(node_y, at + 1)]
        shift = shift_b[here, :]
        sums = remap_parts(
            rho[here, :], ene[here, :], spx[here, :], spy[here, :],
            wide(zed, pl.multiple_of(at + PAD, G)), pre[here, :], lim[here, :], near,
            jnp.concatenate([shift, shift], axis=1), inner, left, right,
        )
        for f in range(4):
            to_left[g, f] = sums[f][:, :TILE]
            to_right[g, f] = sums[f][:, TILE:]
        return carry

    def over(first, last, step):
        lax.fori_loop(first, last, step, None, unroll=min(4, last - first))

    def remote(source, target, send_sem, recv_sem, column, level=gy):
        return pltpu.make_async_remote_copy(
            src_ref=source, dst_ref=target, send_sem=send_sem, recv_sem=recv_sem,
            device_id=(column, level), device_id_type=MESH,
        )

    parts = []
    sends = []
    around, onward = [], []

    def send_part(first, last, detour=False):
        i = len(parts)
        parts.append((first, last))
        there = pl.ds(first, last - first)
        go_right = remote(
            to_right.at[there], from_left.at[there], bulk_send.at[0, i], bulk_recv.at[0, i], right_x
        )
        go_left = remote(
            to_left.at[there], from_right.at[there], bulk_send.at[1, i], bulk_recv.at[1, i], left_x
        )
        sends.extend((go_right, go_left))
        if detour:
            k = len(around)
            stop = passing.at[k, pl.ds(0, last - first)]
            around.append(remote(to_right.at[there], stop, bulk_send.at[0, i], relay_recv.at[k], RELAY))
            onward.append(remote(stop, from_left.at[there], relay_send.at[k], bulk_recv.at[0, i], 0))
            pl.when(is_last)(lambda: around[k].start())
            pl.when(jnp.logical_not(is_last))(lambda: go_right.start())
        else:
            go_right.start()
        go_left.start()

    def send_run(first, last):
        extra = DETOURS.get(first, 0)
        if extra:
            send_part(first, first + extra, True)
        if first + extra < last:
            send_part(first + extra, last)

    filler = jnp.ones((G, TILE), jnp.float32)
    for ref in (zed, pl_x, pr_x, pl_y, pu_y):
        for half in range(2):
            ref[half, 0:G, :] = filler
            ref[half, ROWS + PAD : ROWS + PAD + G, :] = filler

    small_loads[0].wait()
    shift_row = shift_ref[...]
    shift_b[...] = jnp.transpose(jnp.broadcast_to(shift_row, (ROWS, ROWS)))

    for load in loads[0] + loads[1]:
        load.wait()
    derive(15)
    over(0, 6, derive)

    for half in range(2):
        for k, ref in enumerate((zed, pl_x, pr_x, pl_y)):
            outer[4 * half + k : 4 * half + k + 1, :] = ref[half, ROWS + PAD - 1 : ROWS + PAD, :]
        for k, ref in enumerate((zed, pl_x, pr_x, pu_y)):
            outer[8 + 4 * half + k : 8 + 4 * half + k + 1, :] = ref[half, PAD : PAD + 1, :]
    outer_turned = jnp.transpose(
        jnp.concatenate([outer[0:16, :], jnp.zeros((ROWS - 16, TILE), jnp.float32)], axis=0)
    )
    outer[16:24, :] = outer_turned[0:8, :]
    outer[24:32, :] = outer_turned[120:128, :]

    over(1, 6, nodes)
    over(1, 5, cells)


    beside_count = has_up.astype(jnp.int32) + has_down.astype(jnp.int32)
    met = 2 + beside_count + jnp.where(is_last | is_relay, 1, 0) + jnp.where(is_last, beside_count, 0)
    pl.semaphore_wait(barrier, met)

    row_copies = (
        remote(outer, from_down, row_send.at[0], row_recv.at[0], gx, up_y),
        remote(outer, from_up, row_send.at[1], row_recv.at[1], gx, down_y),
    )
    straight = (
        remote(outer.at[24:32, :], corner_ld, corner_send.at[0], corner_recv.at[0], right_x, up_y),
        remote(outer.at[24:32, :], corner_lu, corner_send.at[1], corner_recv.at[1], right_x, down_y),
    )

    def beside(copies, flags, act):
        for copy, flag in zip(copies, flags, strict=True):

            @pl.when(flag)
            def _(copy=copy):
                act(copy)

    def begin(copy):
        copy.start()

    def has_come(copy):
        copy.wait_recv()

    def has_gone(copy):
        copy.wait_send()

    send_part(1, 3, True)
    beside(row_copies, (has_up, has_down), begin)
    send_part(3, 5)
    pl.when(is_last)(lambda: beside(straight, (has_up, has_down), begin))

    for load in loads[2] + small_loads[1:]:
        load.wait()

    packed_l = jnp.zeros((ROWS, TILE), jnp.float32)
    packed_r = jnp.zeros((ROWS, TILE), jnp.float32)
    for f, ref in enumerate((rho, ene, spx, spy, mat, lim)):
        first = ref[:, :TILE].astype(jnp.float32)
        last = ref[:, TILE:].astype(jnp.float32)
        inside = (lanes >= 4 * f) & (lanes < 4 * f + 4)
        packed_l = jnp.where(inside, pltpu.roll(first, 4 * f, 1) if f else first, packed_l)
        packed_r = jnp.where(inside, pltpu.roll(last, 4 * f + 4, 1), packed_r)
    seam_out_l[...] = jnp.transpose(packed_l)[0:24, :]
    seam_out_r[...] = jnp.transpose(packed_r)[0:24, :]

    seam_copies = (
        remote(seam_out_r, seam_in_l, seam_send.at[0], seam_recv.at[0], right_x),
        remote(seam_out_l, seam_in_r, seam_send.at[1], seam_recv.at[1], left_x),
    )
    for copy in seam_copies:
        copy.start()

    for i, (first, last) in enumerate(RUNS[1:3]):
        top = min(last + 1, 15)
        over(first + 1, top, derive)
        over(first + 1, last + 1, nodes)
        over(first, last, cells)
        send_run(first, last)
    over(14, 15, derive)
    over(14, 16, nodes)
    over(13, 15, cells)
    send_run(13, 15)

    @pl.when(jnp.logical_not(has_down))
    def _():
        from_down[...] = jnp.zeros_like(from_down)
        corner_ld[...] = jnp.zeros_like(corner_ld)
        corner_rd[...] = jnp.zeros_like(corner_rd)

    @pl.when(jnp.logical_not(has_up))
    def _():
        from_up[...] = jnp.zeros_like(from_up)
        corner_lu[...] = jnp.zeros_like(corner_lu)
        corner_ru[...] = jnp.zeros_like(corner_ru)

    beside(row_copies, (has_down, has_up), has_come)
    onward_right = (
        remote(from_down.at[24:32, :], corner_ld, corner_send.at[0], corner_recv.at[0], right_x),
        remote(from_up.at[24:32, :], corner_lu, corner_send.at[1], corner_recv.at[1], right_x),
    )
    onward_left = (
        remote(from_down.at[16:24, :], corner_rd, corner_send.at[2], corner_recv.at[2], left_x),
        remote(from_up.at[16:24, :], corner_ru, corner_send.at[3], corner_recv.at[3], left_x),
    )
    pl.when(jnp.logical_not(is_last))(lambda: beside(onward_right, (has_down, has_up), begin))
    beside(onward_left, (has_down, has_up), begin)
    below = from_down[0:8, :]
    above = from_up[8:16, :]
    for half in range(2):
        for k, ref in enumerate((zed, pl_x, pr_x, pl_y)):
            ref[half, PAD - 1 : PAD, :] = below[4 * half + k : 4 * half + k + 1, :]
        for k, ref in enumerate((zed, pl_x, pr_x, pu_y)):
            ref[half, ROWS + PAD : ROWS + PAD + 1, :] = above[4 * half + k : 4 * half + k + 1, :]
    nodes(0)
    nodes(16)
    cells(0)
    cells(15)
    send_run(0, 1)
    send_run(15, 16)

    @pl.when(is_relay)
    def _():
        for arrival, departure in zip(around, onward, strict=True):
            arrival.wait_recv()
            departure.start()


    turn_pairs = jnp.where(owners_ref[...] == gx, lax.bitwise_and(dest_ref[...], 1), -1).astype(jnp.float32)
    turn_row = jnp.zeros((8, ROWS), jnp.float32)
    for j in range(2):
        pick = jnp.where(TILE * j + rows == 2 * lanes, 1.0, 0.0)
        turn_row += jnp.dot(
            jnp.broadcast_to(turn_pairs[j : j + 1], (8, TILE)), pick, preferred_element_type=jnp.float32
        )
    turn_row = turn_row[0:1]
    turn_b[...] = jnp.transpose(jnp.broadcast_to(turn_row, (ROWS, ROWS)))
    for copy in seam_copies:
        copy.wait_recv()
    beside(onward_right + onward_left, (has_down, has_up) * 2, has_come)

    sub8 = lax.broadcasted_iota(jnp.int32, (8, TILE), 0)
    lane8 = lax.broadcasted_iota(jnp.int32, (8, TILE), 1)

    def turned(x, by):
        return pltpu.roll(x, by % 8, 0) if by % 8 else x

    def seam_field(f):
        at, off = 8 * (f // 2), 4 * (f % 2)
        slots = []
        for before, after in ((seam_in_l, seam_out_l), (seam_out_r, seam_in_r)):
            head = turned(before[at : at + 8, :], 8 - off)
            tail = turned(after[at : at + 8, :], 4 - off + 8)
            slots.append(jnp.where(sub8 < 4, head, tail))
        return jnp.concatenate(slots, axis=0)

    def seam_outer(before_l, after_l, before_r, after_r, lane):
        slots = [
            jnp.where(sub8 < 4, turned(before[...], 4)[:, lane + 4 : lane + 5], turned(after[...], 4)[:, lane : lane + 1])
            for before, after in ((before_l, after_l), (before_r, after_r))
        ]
        return jnp.concatenate(slots, axis=0)

    density, energy, speed_x, speed_y, material, limiter = [seam_field(f) for f in range(6)]
    impedance, pressure = cell_state(density, energy, material)
    push_x = impedance * speed_x
    push_y = impedance * speed_y
    first_lane = lax.broadcasted_iota(jnp.int32, (16, ROWS), 1)
    at_first = first_lane == 0
    at_last = first_lane == ROWS - 1

    lower = (corner_ld, from_down.at[16:24, :], from_down.at[24:32, :], corner_rd)
    upper = (corner_lu, from_up.at[16:24, :], from_up.at[24:32, :], corner_ru)
    mine_l = (impedance, push_x + pressure, push_x - pressure, push_y + pressure)
    mine_u = (impedance, push_x + pressure, push_x - pressure, push_y - pressure)
    under = [jnp.where(at_first, seam_outer(*lower, k), pltpu.roll(x, 1, 1)) for k, x in enumerate(mine_l)]
    over_it = [
        jnp.where(at_last, seam_outer(*upper, 8 + k), pltpu.roll(x, ROWS - 1, 1)) for k, x in enumerate(mine_u)
    ]

    def seam_left(x):
        return pltpu.roll(x, 1, 0)

    def seam_right(x):
        return pltpu.roll(x, 15, 0)

    low = node_speed(under, mine_u, seam_left)
    high = node_speed(mine_l, over_it, seam_left)
    sub16 = lax.rem(lax.broadcasted_iota(jnp.int32, (16, ROWS), 0), 8)
    sums = remap_parts(
        density, energy, speed_x, speed_y, impedance, pressure, limiter, low + high,
        jnp.broadcast_to(shift_row, (16, ROWS)), (sub16 >= 2) & (sub16 < 6), seam_left, seam_right,
    )
    stay = turn_row == 0.0
    goes_right = turn_row == 1.0
    goes_left = turn_row == -1.0
    pieces = []
    for f in range(4):
        at_left, at_right = sums[f][0:8], sums[f][8:16]
        moved = jnp.where(goes_right, at_left, jnp.where(goes_left, at_right, 0.0))
        pieces.append(jnp.where(sub8 < 4, moved, jnp.where(stay, at_left, 0.0)))
        pieces.append(jnp.where(sub8 < 4, jnp.where(stay, at_right, 0.0), moved))
    rim[...] = jnp.transpose(jnp.concatenate(pieces + [jnp.zeros((64, ROWS), jnp.float32)], axis=0))

    near_edge = (lane8 < 3) | (lane8 >= TILE - 2)

    def prepare(g, carry):
        here = pl.ds(pl.multiple_of(g * G, G), G)
        turn = turn_b[here, :]
        edge = rim[here, :]
        for f in range(4):
            first, second = to_left[g, f], to_right[g, f]
            for half in range(2):
                q = 2 * f + half
                if half == 0:
                    value = jnp.where(turn == 0.0, first, jnp.where(turn == 1.0, 0.0, second))
                else:
                    value = jnp.where(turn == 0.0, second, jnp.where(turn == 1.0, first, 0.0))
                extra = pltpu.roll(edge, (2 * TILE - 8 * q - 4) % TILE, 1)
                out_ref[f, 0, here, half * TILE : (half + 1) * TILE] = value + jnp.where(near_edge, extra, 0.0)
        return carry

    def finish(g, carry=None):
        here = pl.ds(pl.multiple_of(g * G, G), G)
        turn = turn_b[here, :]
        for f in range(4):
            out_ref[f, 0, here, :TILE] += jnp.where(turn == 1.0, from_left[g, f], 0.0)
            out_ref[f, 0, here, TILE:] += jnp.where(turn == -1.0, from_right[g, f], 0.0)
        return carry

    over(0, 16, prepare)

    for i, (first, last) in enumerate(parts):
        sends[2 * i].wait_recv()
        sends[2 * i + 1].wait_recv()
        over(first, last, finish)

    beside(row_copies, (has_up, has_down), has_gone)
    beside(onward_left, (has_down, has_up), has_gone)
    pl.when(is_last)(lambda: beside(straight, (has_up, has_down), has_gone))
    pl.when(jnp.logical_not(is_last))(lambda: beside(onward_right, (has_down, has_up), has_gone))
    for copy in (*seam_copies, *sends):
        copy.wait_send()

    @pl.when(is_relay)
    def _():
        for departure in onward:
            departure.wait_send()


def on_device(n_gx, n_gy, density, velocity, energy, material, limiter, owners, dest_tile, tile_shift):
    dma = pltpu.SemaphoreType.DMA
    f32 = jnp.float32
    block = pltpu.VMEM((ROWS, COLS), f32)
    padded = pltpu.VMEM((2, ROWS + 2 * PAD, TILE), f32)
    tiles = pltpu.VMEM((ROWS // G, 4, G, TILE), f32)
    square = pltpu.VMEM((ROWS, TILE), f32)
    small = pltpu.VMEM((8, TILE), f32)
    seam = pltpu.VMEM((24, ROWS), f32)
    outer = pltpu.VMEM((32, TILE), f32)
    any_space = pl.BlockSpec(memory_space=pltpu.HBM)
    vmem = pl.BlockSpec(memory_space=pltpu.VMEM)
    return pl.pallas_call(
        functools.partial(kernel, n_gx, n_gy),
        out_shape=pltpu.VMEM((4, 1, ROWS, COLS), f32),
        in_specs=[any_space] * 8,
        out_specs=vmem,
        scratch_shapes=[
            pltpu.VMEM((2, TILE), jnp.int32), pltpu.VMEM((2, TILE), jnp.int32), pltpu.VMEM((1, ROWS), f32),
            block, block, block, block,
            pltpu.VMEM((ROWS, COLS), jnp.int32), pltpu.VMEM((ROWS, COLS), jnp.int32),
            padded, block, padded, padded, padded, padded, padded, padded, square, square,
            tiles, tiles, tiles, tiles,
            outer, outer, outer, small, small, small, small, seam, seam, seam, seam, square, pltpu.VMEM((len(DETOURS), 4, 4, G, TILE), f32),
            dma((3, 9)), dma((2, 10)), dma((2, 10)),
            dma((2,)), dma((2,)), dma((4,)), dma((4,)), dma((2,)), dma((2,)),
            dma((len(DETOURS),)), dma((len(DETOURS),)),
        ],
        compiler_params=pltpu.CompilerParams(
            collective_id=0, has_side_effects=True, vmem_limit_bytes=58 * 1024 * 1024
        ),
    )(
        density, velocity, energy, material, limiter,
        owners.reshape(2, TILE), dest_tile.reshape(2, TILE), tile_shift,
    )


def solution(mesh):
    placed = (
        P(None, "gy", "gx"),
        P(None, None, "gy", "gx"),
        P(None, "gy", "gx"),
        P(None, "gy", "gx"),
        P(None, "gy", "gx"),
        P(("gx", "gy")),
        P(("gx", "gy")),
        P(None, "gy"),
    )
    return jax.shard_map(
        functools.partial(on_device, mesh.shape["gx"], mesh.shape["gy"]),
        mesh=mesh, in_specs=placed, out_specs=P(None, None, "gy", "gx"), check_vma=False,
    )
```

```python
import functools

import jax
import jax.numpy as jnp
from jax import lax
from jax.experimental import pallas as pl
from jax.experimental.pallas import tpu as pltpu
from jax.sharding import PartitionSpec as P

MESH = pl.DeviceIdType.MESH
TILE = 128
ROWS = 128
COLS = 256
PAD = 8
G = 8
time_step = 0.05

RUNS = ((1, 5), (5, 9), (9, 13), (13, 15))
EARLY = 6
DETOURS = {1: 2, 5: 2, 9: 2}
RELAY = 3


def by_material(material, first, second, third):
    return jnp.where(material == 0, first, jnp.where(material == 1, second, third))


def cell_state(density, energy, material):
    pressure = by_material(material, 0.4, 2.0 / 3.0, 2.0) * density * energy
    squared = by_material(material, 0.56, 10.0 / 9.0, 6.0) * energy
    return density * jnp.sqrt(squared), pressure


def node_speed(low, high, left):
    weight = low[0] + high[0]
    from_left = low[1] + high[1]
    from_right = low[2] + high[2]
    along_y = low[3] + high[3]
    scale = 1.0 / (left(weight) + weight)
    return (left(from_left) + from_right) * scale, (left(along_y) + along_y) * scale


def remap_parts(density, energy, speed_x, speed_y, impedance, pressure, limiter, nodes, shift, mask, left, right):
    low_x, low_y, high_x, high_y = nodes
    edge_x = low_x + high_x
    edge_y = low_y + high_y
    turn_y = high_y - low_y
    square = low_x * low_x + high_x * high_x + low_y * low_y + high_y * high_y
    next_x = right(edge_x)
    sum_x = edge_x + next_x
    sum_y = edge_y + right(edge_y)
    volume_rate = 0.5 * ((next_x - edge_x) + (turn_y + right(turn_y)))
    relaxation = (square + right(square)) - speed_x * sum_x - speed_y * sum_y
    half = 0.5 * impedance
    work = half * relaxation - pressure * volume_rate
    left_move = (0.5 * time_step) * edge_x
    right_move = (0.5 * time_step) * next_x
    scale = 1.0 / (1.0 + (right_move - left_move))
    total = density * (energy + 0.5 * (speed_x * speed_x + speed_y * speed_y))
    conserved = (
        density,
        density * speed_x + (time_step * half) * (sum_x - 4.0 * speed_x),
        density * speed_y + (time_step * half) * (sum_y - 4.0 * speed_y),
        total + time_step * work,
    )
    reach = jnp.where(limiter == 1, 2.0, 1.0)
    left_pos = shift + left_move
    right_pos = 1.0 + shift + right_move
    centre = 0.5 * (left_pos + right_pos)
    low_own = jnp.maximum(left_pos, 0.0)
    high_own = jnp.minimum(right_pos, 1.0)
    span_own = jnp.where(mask, jnp.maximum(high_own - low_own, 0.0), 0.0)
    offset_own = 0.5 * (high_own + low_own) - centre
    low_next = jnp.maximum(left_pos, 1.0)
    high_next = jnp.minimum(right_pos, 2.0)
    span_next = jnp.where(mask, jnp.maximum(high_next - low_next, 0.0), 0.0)
    offset_next = 0.5 * (high_next + low_next) - centre
    sums = []
    for field in conserved:
        value = field * scale
        back = value - left(value)
        fore = right(back)
        half_sum = 0.5 * (back + fore)
        limit = reach * jnp.minimum(jnp.abs(back), jnp.abs(fore))
        slope = jnp.where(back * fore > 0.0, jnp.maximum(jnp.minimum(half_sum, limit), -limit), 0.0)
        part_own = span_own * (value + slope * offset_own)
        part_next = span_next * (value + slope * offset_next)
        sums.append(part_own + left(part_next))
    return sums


def kernel(
    n_gx, n_gy,
    density_in, velocity_in, energy_in, material_in, limiter_in, owners_in, dest_in, shift_in, out_ref,
    owners_ref, dest_ref, shift_ref, rho, spx, spy, ene, mat, lim, zed, pre, pl_x, pr_x, pl_y, pu_y, node_x, node_y, shift_b, turn_b,
    to_left, to_right, from_left, from_right, outer, from_down, from_up, corner_ld, corner_lu, corner_rd, corner_ru,
    seam_out_l, seam_out_r, seam_in_l, seam_in_r, rim, passing,
    in_sem, bulk_send, bulk_recv, row_send, row_recv, corner_send, corner_recv, seam_send, seam_recv, relay_send, relay_recv,
):
    gx = lax.axis_index("gx")
    gy = lax.axis_index("gy")
    right_x = lax.rem(gx + 1, n_gx)
    left_x = lax.rem(gx + n_gx - 1, n_gx)
    up_y = lax.rem(gy + 1, n_gy)
    down_y = lax.rem(gy + n_gy - 1, n_gy)

    small_loads = [
        pltpu.make_async_copy(source, target, in_sem.at[0, 6 + k])
        for k, (source, target) in enumerate(((shift_in, shift_ref), (owners_in, owners_ref), (dest_in, dest_ref)))
    ]
    fields = (
        (density_in.at[0], rho),
        (energy_in.at[0], ene),
        (material_in.at[0], mat),
        (velocity_in.at[0, 0], spx),
        (velocity_in.at[1, 0], spy),
        (limiter_in.at[0], lim),
    )
    slabs = (pl.ds(0, EARLY * G), pl.ds(ROWS - G, G), pl.ds(EARLY * G, ROWS - G - EARLY * G))
    loads = [
        [pltpu.make_async_copy(source.at[part, :], target.at[part, :], in_sem.at[i, k]) for k, (source, target) in enumerate(fields)]
        for i, part in enumerate(slabs)
    ]
    for load in small_loads[:1] + loads[0] + loads[1] + loads[2] + small_loads[1:]:
        load.start()

    has_up = gy < n_gy - 1
    has_down = gy > 0
    barrier = pltpu.get_barrier_semaphore()

    def greet(column, level):
        pl.semaphore_signal(barrier, inc=1, device_id=(column, level), device_id_type=MESH)

    greet(left_x, gy)
    greet(right_x, gy)
    pl.when(has_up)(lambda: greet(gx, up_y))
    pl.when(has_down)(lambda: greet(gx, down_y))
    is_last = gx == n_gx - 1
    is_relay = gx == RELAY
    pl.when(is_relay)(lambda: greet(n_gx - 1, gy))

    @pl.when(gx == 0)
    def _():
        greet(RELAY, gy)
        pl.when(has_up)(lambda: greet(left_x, up_y))
        pl.when(has_down)(lambda: greet(left_x, down_y))


    lanes = lax.broadcasted_iota(jnp.int32, (ROWS, TILE), 1)
    rows = lax.broadcasted_iota(jnp.int32, (ROWS, TILE), 0)

    def wide(ref, start):
        return jnp.concatenate([ref[0, pl.ds(start, G), :], ref[1, pl.ds(start, G), :]], axis=1)

    def keep(ref, start, value):
        ref[0, pl.ds(start, G), :] = value[:, :TILE]
        ref[1, pl.ds(start, G), :] = value[:, TILE:]

    def left(x):
        return pltpu.roll(x, 1, 1)

    def right(x):
        return pltpu.roll(x, COLS - 1, 1)

    def derive(g, carry=None):
        at = pl.multiple_of(g * G, G)
        density = rho[pl.ds(at, G), :]
        speed_x = spx[pl.ds(at, G), :]
        speed_y = spy[pl.ds(at, G), :]
        impedance, pressure = cell_state(density, ene[pl.ds(at, G), :], mat[pl.ds(at, G), :])
        pad_at = pl.multiple_of(at + PAD, G)
        keep(zed, pad_at, impedance)
        pre[pl.ds(at, G), :] = pressure
        push_x = impedance * speed_x
        push_y = impedance * speed_y
        keep(pl_x, pad_at, push_x + pressure)
        keep(pr_x, pad_at, push_x - pressure)
        keep(pl_y, pad_at, push_y + pressure)
        keep(pu_y, pad_at, push_y - pressure)
        return carry

    def nodes(g, carry=None):
        at = pl.multiple_of(g * G, G)
        low = [wide(ref, at + PAD - 1) for ref in (zed, pl_x, pr_x, pl_y)]
        high = [wide(ref, pl.multiple_of(at + PAD, G)) for ref in (zed, pl_x, pr_x, pu_y)]
        x, y = node_speed(low, high, left)
        keep(node_x, at, x)
        keep(node_y, at, y)
        return carry

    inner = lax.broadcasted_iota(jnp.int32, (G, COLS), 1)
    inner = (inner >= 2) & (inner < COLS - 2)

    def cells(g, carry=None):
        at = pl.multiple_of(g * G, G)
        here = pl.ds(at, G)
        near = [wide(node_x, at), wide(node_y, at), wide(node_x, at + 1), wide(node_y, at + 1)]
        shift = shift_b[here, :]
        sums = remap_parts(
            rho[here, :], ene[here, :], spx[here, :], spy[here, :],
            wide(zed, pl.multiple_of(at + PAD, G)), pre[here, :], lim[here, :], near,
            jnp.concatenate([shift, shift], axis=1), inner, left, right,
        )
        for f in range(4):
            to_left[f, here, :] = sums[f][:, :TILE]
            to_right[f, here, :] = sums[f][:, TILE:]
        return carry

    def over(first, last, step):
        lax.fori_loop(first, last, step, None, unroll=min(4, last - first))

    def remote(source, target, send_sem, recv_sem, column, level=gy):
        return pltpu.make_async_remote_copy(
            src_ref=source, dst_ref=target, send_sem=send_sem, recv_sem=recv_sem,
            device_id=(column, level), device_id_type=MESH,
        )

    parts = []
    sends = []
    around, onward = [], []

    def send_part(first, last, detour=False):
        i = len(parts)
        parts.append((first, last))
        there = pl.ds(first * G, (last - first) * G)
        go_right = remote(
            to_right.at[:, there, :], from_left.at[:, there, :], bulk_send.at[0, i], bulk_recv.at[0, i], right_x
        )
        go_left = remote(
            to_left.at[:, there, :], from_right.at[:, there, :], bulk_send.at[1, i], bulk_recv.at[1, i], left_x
        )
        sends.extend((go_right, go_left))
        if detour:
            k = len(around)
            stop = passing.at[k, :, pl.ds(0, (last - first) * G), :]
            around.append(remote(to_right.at[:, there, :], stop, bulk_send.at[0, i], relay_recv.at[k], RELAY))
            onward.append(remote(stop, from_left.at[:, there, :], relay_send.at[k], bulk_recv.at[0, i], 0))
            pl.when(is_last & has_down)(lambda: around[k].start())
            pl.when(jnp.logical_not(is_last) & has_down)(lambda: go_right.start())
        else:
            pl.when(has_down)(lambda: go_right.start())
        pl.when(has_up)(lambda: go_left.start())

    def send_run(first, last):
        extra = DETOURS.get(first, 0)
        if extra:
            send_part(first, first + extra, True)
        if first + extra < last:
            send_part(first + extra, last)

    filler = jnp.ones((G, TILE), jnp.float32)
    for ref in (zed, pl_x, pr_x, pl_y, pu_y):
        for half in range(2):
            ref[half, 0:G, :] = filler
            ref[half, ROWS + PAD : ROWS + PAD + G, :] = filler

    small_loads[0].wait()
    shift_row = shift_ref[...]
    shift_b[...] = jnp.transpose(jnp.broadcast_to(shift_row, (ROWS, ROWS)))

    for load in loads[0] + loads[1]:
        load.wait()
    derive(15)
    over(0, 6, derive)

    for half in range(2):
        for k, ref in enumerate((zed, pl_x, pr_x, pl_y)):
            outer[4 * half + k : 4 * half + k + 1, :] = ref[half, ROWS + PAD - 1 : ROWS + PAD, :]
        for k, ref in enumerate((zed, pl_x, pr_x, pu_y)):
            outer[8 + 4 * half + k : 8 + 4 * half + k + 1, :] = ref[half, PAD : PAD + 1, :]
    outer_turned = jnp.transpose(
        jnp.concatenate([outer[0:16, :], jnp.zeros((ROWS - 16, TILE), jnp.float32)], axis=0)
    )
    outer[16:24, :] = outer_turned[0:8, :]
    outer[24:32, :] = outer_turned[120:128, :]

    over(1, 6, nodes)
    over(1, 5, cells)


    beside_count = has_up.astype(jnp.int32) + has_down.astype(jnp.int32)
    met = 2 + beside_count + jnp.where(is_last | is_relay, 1, 0) + jnp.where(is_last, beside_count, 0)
    pl.semaphore_wait(barrier, met)

    row_copies = (
        remote(outer, from_down, row_send.at[0], row_recv.at[0], gx, up_y),
        remote(outer, from_up, row_send.at[1], row_recv.at[1], gx, down_y),
    )
    straight = (
        remote(outer.at[24:32, :], corner_ld, corner_send.at[0], corner_recv.at[0], right_x, up_y),
        remote(outer.at[24:32, :], corner_lu, corner_send.at[1], corner_recv.at[1], right_x, down_y),
    )

    def beside(copies, flags, act):
        for copy, flag in zip(copies, flags, strict=True):

            @pl.when(flag)
            def _(copy=copy):
                act(copy)

    def begin(copy):
        copy.start()

    def has_come(copy):
        copy.wait_recv()

    def has_gone(copy):
        copy.wait_send()

    beside(row_copies, (has_up, has_down), begin)
    pl.when(is_last)(lambda: beside(straight, (has_up, has_down), begin))

    send_part(1, 3, True)
    send_part(3, 5)
    for load in loads[2] + small_loads[1:]:
        load.wait()

    packed_l = jnp.zeros((ROWS, TILE), jnp.float32)
    packed_r = jnp.zeros((ROWS, TILE), jnp.float32)
    for f, ref in enumerate((rho, ene, spx, spy, mat, lim)):
        first = ref[:, :TILE].astype(jnp.float32)
        last = ref[:, TILE:].astype(jnp.float32)
        inside = (lanes >= 4 * f) & (lanes < 4 * f + 4)
        packed_l = jnp.where(inside, pltpu.roll(first, 4 * f, 1) if f else first, packed_l)
        packed_r = jnp.where(inside, pltpu.roll(last, 4 * f + 4, 1), packed_r)
    seam_out_l[...] = jnp.transpose(packed_l)[0:24, :]
    seam_out_r[...] = jnp.transpose(packed_r)[0:24, :]

    seam_copies = (
        remote(seam_out_r, seam_in_l, seam_send.at[0], seam_recv.at[0], right_x),
        remote(seam_out_l, seam_in_r, seam_send.at[1], seam_recv.at[1], left_x),
    )
    for copy in seam_copies:
        copy.start()

    for i, (first, last) in enumerate(RUNS[1:3]):
        top = min(last + 1, 15)
        over(first + 1, top, derive)
        over(first + 1, last + 1, nodes)
        over(first, last, cells)
        send_run(first, last)
    over(14, 15, derive)
    over(14, 16, nodes)
    over(13, 15, cells)
    send_run(13, 15)

    @pl.when(jnp.logical_not(has_down))
    def _():
        from_left[...] = jnp.zeros_like(from_left)

    @pl.when(jnp.logical_not(has_up))
    def _():
        from_right[...] = jnp.zeros_like(from_right)

    @pl.when(jnp.logical_not(has_down))
    def _():
        from_down[...] = jnp.zeros_like(from_down)
        corner_ld[...] = jnp.zeros_like(corner_ld)
        corner_rd[...] = jnp.zeros_like(corner_rd)

    @pl.when(jnp.logical_not(has_up))
    def _():
        from_up[...] = jnp.zeros_like(from_up)
        corner_lu[...] = jnp.zeros_like(corner_lu)
        corner_ru[...] = jnp.zeros_like(corner_ru)

    beside(row_copies, (has_down, has_up), has_come)
    onward_right = (
        remote(from_down.at[24:32, :], corner_ld, corner_send.at[0], corner_recv.at[0], right_x),
        remote(from_up.at[24:32, :], corner_lu, corner_send.at[1], corner_recv.at[1], right_x),
    )
    onward_left = (
        remote(from_down.at[16:24, :], corner_rd, corner_send.at[2], corner_recv.at[2], left_x),
        remote(from_up.at[16:24, :], corner_ru, corner_send.at[3], corner_recv.at[3], left_x),
    )
    pl.when(jnp.logical_not(is_last))(lambda: beside(onward_right, (has_down, has_up), begin))
    beside(onward_left, (has_down, has_up), begin)
    below = from_down[0:8, :]
    above = from_up[8:16, :]
    for half in range(2):
        for k, ref in enumerate((zed, pl_x, pr_x, pl_y)):
            ref[half, PAD - 1 : PAD, :] = below[4 * half + k : 4 * half + k + 1, :]
        for k, ref in enumerate((zed, pl_x, pr_x, pu_y)):
            ref[half, ROWS + PAD : ROWS + PAD + 1, :] = above[4 * half + k : 4 * half + k + 1, :]
    nodes(0)
    nodes(16)
    cells(0)
    cells(15)
    send_run(0, 1)
    send_run(15, 16)

    @pl.when(is_relay & has_down)
    def _():
        for arrival, departure in zip(around, onward, strict=True):
            arrival.wait_recv()
            departure.start()


    turn_pairs = jnp.where(owners_ref[...] == gx, lax.bitwise_and(dest_ref[...], 1), -1).astype(jnp.float32)
    turn_row = jnp.zeros((8, ROWS), jnp.float32)
    for j in range(2):
        pick = jnp.where(TILE * j + rows == 2 * lanes, 1.0, 0.0)
        turn_row += jnp.dot(
            jnp.broadcast_to(turn_pairs[j : j + 1], (8, TILE)), pick, preferred_element_type=jnp.float32
        )
    turn_row = turn_row[0:1]
    turn_b[...] = jnp.transpose(jnp.broadcast_to(turn_row, (ROWS, ROWS)))
    for copy in seam_copies:
        copy.wait_recv()
    beside(onward_right + onward_left, (has_down, has_up) * 2, has_come)

    sub8 = lax.broadcasted_iota(jnp.int32, (8, TILE), 0)
    lane8 = lax.broadcasted_iota(jnp.int32, (8, TILE), 1)

    def turned(x, by):
        return pltpu.roll(x, by % 8, 0) if by % 8 else x

    def seam_field(f):
        at, off = 8 * (f // 2), 4 * (f % 2)
        slots = []
        for before, after in ((seam_in_l, seam_out_l), (seam_out_r, seam_in_r)):
            head = turned(before[at : at + 8, :], 8 - off)
            tail = turned(after[at : at + 8, :], 4 - off + 8)
            slots.append(jnp.where(sub8 < 4, head, tail))
        return jnp.concatenate(slots, axis=0)

    def seam_outer(before_l, after_l, before_r, after_r, lane):
        slots = [
            jnp.where(sub8 < 4, turned(before[...], 4)[:, lane + 4 : lane + 5], turned(after[...], 4)[:, lane : lane + 1])
            for before, after in ((before_l, after_l), (before_r, after_r))
        ]
        return jnp.concatenate(slots, axis=0)

    density, energy, speed_x, speed_y, material, limiter = [seam_field(f) for f in range(6)]
    impedance, pressure = cell_state(density, energy, material)
    push_x = impedance * speed_x
    push_y = impedance * speed_y
    first_lane = lax.broadcasted_iota(jnp.int32, (16, ROWS), 1)
    at_first = first_lane == 0
    at_last = first_lane == ROWS - 1

    lower = (corner_ld, from_down.at[16:24, :], from_down.at[24:32, :], corner_rd)
    upper = (corner_lu, from_up.at[16:24, :], from_up.at[24:32, :], corner_ru)
    mine_l = (impedance, push_x + pressure, push_x - pressure, push_y + pressure)
    mine_u = (impedance, push_x + pressure, push_x - pressure, push_y - pressure)
    under = [jnp.where(at_first, seam_outer(*lower, k), pltpu.roll(x, 1, 1)) for k, x in enumerate(mine_l)]
    over_it = [
        jnp.where(at_last, seam_outer(*upper, 8 + k), pltpu.roll(x, ROWS - 1, 1)) for k, x in enumerate(mine_u)
    ]

    def seam_left(x):
        return pltpu.roll(x, 1, 0)

    def seam_right(x):
        return pltpu.roll(x, 15, 0)

    low = node_speed(under, mine_u, seam_left)
    high = node_speed(mine_l, over_it, seam_left)
    sub16 = lax.rem(lax.broadcasted_iota(jnp.int32, (16, ROWS), 0), 8)
    sums = remap_parts(
        density, energy, speed_x, speed_y, impedance, pressure, limiter, low + high,
        jnp.broadcast_to(shift_row, (16, ROWS)), (sub16 >= 2) & (sub16 < 6), seam_left, seam_right,
    )
    stay = turn_row == 0.0
    goes_right = turn_row == 1.0
    goes_left = turn_row == -1.0
    pieces = []
    for f in range(4):
        at_left, at_right = sums[f][0:8], sums[f][8:16]
        moved = jnp.where(goes_right, at_left, jnp.where(goes_left, at_right, 0.0))
        pieces.append(jnp.where(sub8 < 4, moved, jnp.where(stay, at_left, 0.0)))
        pieces.append(jnp.where(sub8 < 4, jnp.where(stay, at_right, 0.0), moved))
    rim[...] = jnp.transpose(jnp.concatenate(pieces + [jnp.zeros((64, ROWS), jnp.float32)], axis=0))

    near_edge = (lane8 < 3) | (lane8 >= TILE - 2)

    def prepare(g, carry):
        here = pl.ds(pl.multiple_of(g * G, G), G)
        turn = turn_b[here, :]
        edge = rim[here, :]
        for f in range(4):
            first, second = to_left[f, here, :], to_right[f, here, :]
            for half in range(2):
                q = 2 * f + half
                if half == 0:
                    value = jnp.where(turn == 0.0, first, jnp.where(turn == 1.0, 0.0, second))
                else:
                    value = jnp.where(turn == 0.0, second, jnp.where(turn == 1.0, first, 0.0))
                extra = pltpu.roll(edge, (2 * TILE - 8 * q - 4) % TILE, 1)
                out_ref[f, 0, here, half * TILE : (half + 1) * TILE] = value + jnp.where(near_edge, extra, 0.0)
        return carry

    def finish(g, carry=None):
        here = pl.ds(pl.multiple_of(g * G, G), G)
        turn = turn_b[here, :]
        for f in range(4):
            out_ref[f, 0, here, :TILE] += jnp.where(turn == 1.0, from_left[f, here, :], 0.0)
            out_ref[f, 0, here, TILE:] += jnp.where(turn == -1.0, from_right[f, here, :], 0.0)
        return carry

    over(0, 16, prepare)

    for i, (first, last) in enumerate(parts):
        pl.when(has_down)(lambda: sends[2 * i].wait_recv())
        pl.when(has_up)(lambda: sends[2 * i + 1].wait_recv())
        over(first, last, finish)

    beside(row_copies, (has_up, has_down), has_gone)
    beside(onward_left, (has_down, has_up), has_gone)
    pl.when(is_last)(lambda: beside(straight, (has_up, has_down), has_gone))
    pl.when(jnp.logical_not(is_last))(lambda: beside(onward_right, (has_down, has_up), has_gone))
    for copy in seam_copies:
        copy.wait_send()
    for go_right, go_left in zip(sends[0::2], sends[1::2], strict=True):
        pl.when(has_down)(lambda: go_right.wait_send())
        pl.when(has_up)(lambda: go_left.wait_send())

    @pl.when(is_relay & has_down)
    def _():
        for departure in onward:
            departure.wait_send()


def on_device(n_gx, n_gy, density, velocity, energy, material, limiter, owners, dest_tile, tile_shift):
    dma = pltpu.SemaphoreType.DMA
    f32 = jnp.float32
    block = pltpu.VMEM((ROWS, COLS), f32)
    padded = pltpu.VMEM((2, ROWS + 2 * PAD, TILE), f32)
    tiles = pltpu.VMEM((4, ROWS, TILE), f32)
    square = pltpu.VMEM((ROWS, TILE), f32)
    small = pltpu.VMEM((8, TILE), f32)
    seam = pltpu.VMEM((24, ROWS), f32)
    outer = pltpu.VMEM((32, TILE), f32)
    any_space = pl.BlockSpec(memory_space=pltpu.HBM)
    vmem = pl.BlockSpec(memory_space=pltpu.VMEM)
    return pl.pallas_call(
        functools.partial(kernel, n_gx, n_gy),
        out_shape=pltpu.VMEM((4, 1, ROWS, COLS), f32),
        in_specs=[any_space] * 8,
        out_specs=vmem,
        scratch_shapes=[
            pltpu.VMEM((2, TILE), jnp.int32), pltpu.VMEM((2, TILE), jnp.int32), pltpu.VMEM((1, ROWS), f32),
            block, block, block, block,
            pltpu.VMEM((ROWS, COLS), jnp.int32), pltpu.VMEM((ROWS, COLS), jnp.int32),
            padded, block, padded, padded, padded, padded, padded, padded, square, square,
            tiles, tiles, tiles, tiles,
            outer, outer, outer, small, small, small, small, seam, seam, seam, seam, square, pltpu.VMEM((len(DETOURS), 4, 4 * G, TILE), f32),
            dma((3, 9)), dma((2, 10)), dma((2, 10)),
            dma((2,)), dma((2,)), dma((4,)), dma((4,)), dma((2,)), dma((2,)),
            dma((len(DETOURS),)), dma((len(DETOURS),)),
        ],
        compiler_params=pltpu.CompilerParams(
            collective_id=0, has_side_effects=True, vmem_limit_bytes=58 * 1024 * 1024
        ),
    )(
        density, velocity, energy, material, limiter,
        owners.reshape(2, TILE), dest_tile.reshape(2, TILE), tile_shift,
    )


def solution(mesh):
    placed = (
        P(None, "gy", "gx"),
        P(None, None, "gy", "gx"),
        P(None, "gy", "gx"),
        P(None, "gy", "gx"),
        P(None, "gy", "gx"),
        P(("gx", "gy")),
        P(("gx", "gy")),
        P(None, "gy"),
    )
    return jax.shard_map(
        functools.partial(on_device, mesh.shape["gx"], mesh.shape["gy"]),
        mesh=mesh, in_specs=placed, out_specs=P(None, None, "gy", "gx"), check_vma=False,
    )
```
